256 devices in a mesh: row: 32 (over z, y_lo, core), col: 8 (over y_hi, x).
Axes of the slice: x: 4, y: 4 (y_hi: 2, y_lo: 2; y = y_hi * 2 + y_lo), z: 8, core: 2. Of those that a mesh axis runs over, the one named last changes fastest.
Arguments:
- features: bfloat16 [131072, 128], P(('row', 'col')), may hold values from -6 to 6
- self_weight: bfloat16 [128, 256], replicated, may hold values from -0.5 to 0.5
- neigh_weight: bfloat16 [128, 256], replicated, may hold values from -0.5 to 0.5
- block_row: int32 [32, 8, 512], P('row', 'col'), may hold values from 0 to 63, as said below
- block_col: int32 [32, 8, 512], P('row', 'col'), may hold values from 0 to 255
- block_count: int32 [32, 8], P('row', 'col'), may hold values from 64 to 512, as said below
- edge_weight: int32 [32, 8, 512, 4096], P('row', 'col'), may hold values from 0 to 1, as said below
- train_mask: int32 [131072], P(('row', 'col')), may hold values 0 or 1
- out_cotangent: bfloat16 [131072, 256], P(('row', 'col')), may hold values from -6 to 6
Outputs:
- hidden: bfloat16 [131072, 256], P(('row', 'col'))
- grad_input: bfloat16 [131072, 128], P(('row', 'col'))
- grad_self: float32 [128, 256], replicated
- grad_neigh: float32 [128, 256], replicated
The draws below stay inside these ranges and needn't reach their ends.
Inputs may be any that keep to these rules, and one draw needn't show every extreme that they name: block_row is s for every slot s < 64, so every block row of every tile holds a live block. `block_count`: one tile in every draw has exactly 512 live slots. `edge_weight`: in every slot s < 64 the block's diagonal entries are 1.
All inputs are finite; a program needn't handle non-finite values. No bound on the sum of `train_mask` on one device may be relied on, other than what follows from the above.
Results may differ from the reference program's by a relative error of at most 0.019.
Values may be sent and summed in bfloat16 or wider, within the bound.
A program may use at most 128 MiB of HBM per device.

```python
import jax
import jax.numpy as jnp
from jax import lax

F = 128
H = 256
BLOCK = 64
ND = 512
MAXB = 512
GRID_R = 32
GRID_C = 8
NODES = 131072
BROWS = 64
BCOLS = 256


def draw_block_row(key, part):
    key = jax.random.fold_in(key, 11)
    slots = jnp.arange(MAXB).astype(jnp.int32)[None, None, :]
    random_rows = jax.random.randint(key, (GRID_R, GRID_C, MAXB), 0, BROWS).astype(jnp.int32)
    return jnp.where(slots < BROWS, slots, random_rows)


def draw_block_col(key, part):
    key = jax.random.fold_in(key, 23)
    slots = jnp.arange(MAXB).astype(jnp.int32)[None, None, :]
    random_cols = jax.random.randint(key, (GRID_R, GRID_C, MAXB), 0, BCOLS).astype(jnp.int32)
    return jnp.where(slots == 0, BCOLS - 1, random_cols)


def draw_block_count(key, part):
    key = jax.random.fold_in(key, 37)
    first, second = jax.random.split(key)
    spare = MAXB - BROWS
    extra = jax.random.randint(first, (GRID_R, GRID_C), 0, spare + 1).astype(jnp.int32)
    counts = BROWS + extra * extra // spare
    chosen = jax.random.randint(second, (), 0, GRID_R * GRID_C).astype(jnp.int32)
    flat = jnp.arange(GRID_R * GRID_C).astype(jnp.int32).reshape(GRID_R, GRID_C)
    return jnp.where(flat == chosen, MAXB, counts).astype(jnp.int32)


def draw_edge_weight(key, part):
    key = jax.random.fold_in(key, 47)
    picks = jax.random.randint(key, (GRID_R, GRID_C, MAXB, BLOCK * BLOCK), 0, 32).astype(jnp.int32)
    edges = (picks == 0).astype(jnp.int32)
    cells = jnp.arange(BLOCK * BLOCK).astype(jnp.int32)
    on_diagonal = (cells // BLOCK == cells % BLOCK)[None, None, None, :]
    slots = jnp.arange(MAXB).astype(jnp.int32)[None, None, :, None]
    return jnp.where(on_diagonal & (slots < BROWS), 1, edges).astype(jnp.int32)


def touch_ends(array, key, smallest, top_value):
    extent = array.shape
    spot = [jax.random.randint(jax.random.fold_in(key, axis), (), 0, extent[axis]) for axis in range(len(extent))]
    array = array.at[tuple(spot)].set(smallest)
    longest = extent.index(max(extent))
    spot[longest] = (spot[longest] + 1) % extent[longest]
    return array.at[tuple(spot)].set(top_value)


def shard_levels(rng, extent, shards, least, largest):
    loudness, own = 1.0, jax.random.fold_in(rng, 6)
    for dim, blocks in shards:
        heights = jnp.exp(jax.random.uniform(jax.random.fold_in(own, dim), (blocks,), jnp.float32, least / len(shards), largest / len(shards)))
        loudness = loudness * jnp.repeat(heights, extent[dim] // blocks).reshape([-1 if axis == dim else 1 for axis in range(len(extent))])
    return loudness


def noise(rng, dims, scale, bound, cuts=(), held_as=jnp.bfloat16):
    level = shard_levels(rng, dims, cuts, -0.22, 0.18) if cuts else 1.0
    result = jax.random.normal(rng, dims, jnp.float32) * scale * level
    return jnp.minimum(jnp.maximum(result, -bound), bound).astype(held_as)


def setup_inputs(seed: int = 0) -> dict:
    splits = jax.random.split(jax.random.key(seed), 10)
    return {
        "features": noise(splits[0], (NODES, F), 1.0, 6.0, ((0, 256),)),
        "self_weight": noise(splits[1], (F, H), F ** -0.5, 0.5),
        "neigh_weight": noise(splits[2], (F, H), F ** -0.5, 0.5),
        "block_row": draw_block_row(jax.random.fold_in(splits[9], 71), 0),
        "block_col": draw_block_col(jax.random.fold_in(splits[9], 71), 0),
        "block_count": draw_block_count(jax.random.fold_in(splits[9], 71), 0),
        "edge_weight": draw_edge_weight(jax.random.fold_in(splits[9], 71), 0),
        "train_mask": touch_ends((jax.random.randint(splits[7], (NODES,), 0, 4) < 1).astype(jnp.int32), jax.random.fold_in(splits[7], 1), 0, 1),
        "out_cotangent": noise(splits[8], (NODES, H), 1.0, 6.0, ((0, 256),)),
    }


def tile_layout(tile, rows_in, cols_in, count):
    tile_i = tile // GRID_C
    tile_j = tile % GRID_C
    inner = jnp.arange(BLOCK).astype(jnp.int32)
    rows = (tile_i * GRID_C * ND + rows_in[:, None] * BLOCK + inner[None, :]).astype(jnp.int32)
    local = cols_in[:, None] * BLOCK + inner[None, :]
    cols = (((local // ND) * GRID_C + tile_j) * ND + local % ND).astype(jnp.int32)
    valid = (jnp.arange(MAXB).astype(jnp.int32) < count).astype(jnp.float32)
    return rows, cols, valid


def reference(features, self_weight, neigh_weight, block_row, block_col, block_count, edge_weight, train_mask, out_cotangent):
    tiles = jnp.arange(GRID_R * GRID_C).astype(jnp.int32)
    rows_all = block_row.reshape(GRID_R * GRID_C, MAXB)
    cols_all = block_col.reshape(GRID_R * GRID_C, MAXB)
    counts = block_count.reshape(GRID_R * GRID_C)
    weights_all = edge_weight.reshape(GRID_R * GRID_C, MAXB, BLOCK, BLOCK)
    feats32 = features.astype(jnp.float32)

    def forward_tile(carry, item):
        raw, degree = carry
        tile, rows_in, cols_in, count, wts = item
        rows, cols, valid = tile_layout(tile, rows_in, cols_in, count)
        wmat = wts.astype(jnp.float32) * valid[:, None, None]
        prod = jnp.einsum("sab,sbd->sad", wmat, feats32[cols])
        raw = raw.at[rows.reshape(-1)].add(prod.reshape(-1, F))
        degree = degree.at[rows.reshape(-1)].add(jnp.sum(wmat, axis=2).reshape(-1))
        return (raw, degree), None

    init = (jnp.zeros((NODES, F), jnp.float32), jnp.zeros((NODES,), jnp.float32))
    (raw, degree), _ = lax.scan(forward_tile, init, (tiles, rows_all, cols_all, counts, weights_all))
    agg = (raw / degree[:, None]).astype(jnp.bfloat16)
    pre = jnp.dot(features, self_weight, preferred_element_type=jnp.float32) + jnp.dot(agg, neigh_weight, preferred_element_type=jnp.float32)
    hidden = jax.nn.silu(pre).astype(jnp.bfloat16)
    sig = jax.nn.sigmoid(pre)
    dpre = (out_cotangent.astype(jnp.float32) * train_mask.astype(jnp.float32)[:, None] * sig * (1.0 + pre * (1.0 - sig))).astype(jnp.bfloat16)
    grad_self = jnp.dot(features.T, dpre, preferred_element_type=jnp.float32)
    grad_neigh = jnp.dot(agg.T, dpre, preferred_element_type=jnp.float32)
    scaled = (jnp.dot(dpre, neigh_weight.T, preferred_element_type=jnp.float32) / degree[:, None]).astype(jnp.bfloat16)
    scaled32 = scaled.astype(jnp.float32)
    tile_cols = GRID_R * ND
    inner = jnp.arange(BLOCK).astype(jnp.int32)
    local_all = jnp.arange(tile_cols).astype(jnp.int32)

    def backward_tile(total, item):
        tile, rows_in, cols_in, count, wts = item
        rows, cols, valid = tile_layout(tile, rows_in, cols_in, count)
        wmat = wts.astype(jnp.float32) * valid[:, None, None]
        contrib = jnp.einsum("sab,sad->sbd", wmat, scaled32[rows])
        local = (cols_in[:, None] * BLOCK + inner[None, :]).astype(jnp.int32)
        part = jnp.zeros((tile_cols, F), jnp.float32).at[local.reshape(-1)].add(contrib.reshape(-1, F))
        part = part.astype(jnp.bfloat16).astype(jnp.float32)
        targets = (((local_all // ND) * GRID_C + tile % GRID_C) * ND + local_all % ND).astype(jnp.int32)
        return total.at[targets].add(part), None

    through, _ = lax.scan(backward_tile, jnp.zeros((NODES, F), jnp.float32), (tiles, rows_all, cols_all, counts, weights_all))
    grad_input = (jnp.dot(dpre, self_weight.T, preferred_element_type=jnp.float32) + through).astype(jnp.bfloat16)
    return hidden, grad_input, grad_self, grad_neigh
```

```python
import functools

import jax
import jax.numpy as jnp
from jax import lax
from jax.experimental import pallas as pl
from jax.experimental.pallas import tpu as pltpu
from jax.sharding import PartitionSpec as P

MESH = pl.DeviceIdType.MESH
BF = jnp.bfloat16
F32 = jnp.float32
VMEM = pl.BlockSpec(memory_space=pltpu.VMEM)
SMEM = pl.BlockSpec(memory_space=pltpu.SMEM)
ANY = pl.BlockSpec(memory_space=pl.ANY)
ND = 512
LIMIT = 52 << 20
UNROLL = 16


def place():
    row = lax.axis_index("row")
    return row // 4, (row // 2) % 2, row % 2, lax.axis_index("col")


def greet(targets):
    barrier = pltpu.get_barrier_semaphore()
    for target in targets:
        pl.semaphore_signal(barrier, inc=1, device_id=target, device_id_type=MESH)
    pl.semaphore_wait(barrier, len(targets))


def prep_kernel(cnt, rows, w, zf, zt, deg, pat, dsl):
    i = pl.program_id(0)

    @pl.when(i == 0)
    def _():
        at = lax.broadcasted_iota(jnp.int32, (4096, 128), 0) // 64
        pat[...] = (at == lax.broadcasted_iota(jnp.int32, (4096, 128), 1)).astype(BF)

    lim = cnt[0]
    low = lax.broadcasted_iota(jnp.int32, (32, 128), 1) < 64

    @pl.loop(0, 8)
    def _(g8):
        b = pl.multiple_of(g8 * 8, 8)
        x = w[pl.ds(b, 8), :]
        live = (i * 64 + b + lax.broadcasted_iota(jnp.int32, (8, 4096), 0)) < lim
        y = jnp.where(live, x, 0).astype(F32).reshape(8, 32, 128)
        for h4 in range(2):
            y4 = [y[h4 * 4 + s] for s in range(4)]
            r4 = [pltpu.roll(v, 64, 1) for v in y4]
            z = jnp.concatenate(
                [
                    jnp.where(low, y4[0], r4[2]),
                    jnp.where(low, r4[0], y4[2]),
                    jnp.where(low, y4[1], r4[3]),
                    jnp.where(low, r4[1], y4[3]),
                ],
                0,
            )
            zf[g8 * 2 + h4] = z.astype(BF)
            zt[g8 * 2 + h4] = z.T.astype(BF)

    live = (i * 64 + lax.broadcasted_iota(jnp.int32, (64, 4096), 0)) < lim
    xb = jnp.where(live, w[...], 0).astype(F32).astype(BF)
    dsl[pl.ds(pl.multiple_of(i * 64, 64), 64), :] = jnp.dot(
        xb, pat[...], preferred_element_type=F32
    ).astype(BF)

    @pl.when(i == 7)
    def _():
        hot = (lax.broadcasted_iota(jnp.int32, (64, 512), 0) == rows[...]).astype(F32).astype(BF)
        deg[...] = jnp.dot(hot, dsl[...], preferred_element_type=F32)


def prep(count, rows, w):
    return pl.pallas_call(
        prep_kernel,
        grid=(8,),
        in_specs=[
            SMEM,
            pl.BlockSpec((1, 512), lambda i: (0, 0)),
            pl.BlockSpec((64, 4096), lambda i: (i, 0)),
        ],
        out_specs=[
            pl.BlockSpec((16, 128, 128), lambda i: (i, 0, 0)),
            pl.BlockSpec((16, 128, 128), lambda i: (i, 0, 0)),
            pl.BlockSpec((64, 128), lambda i: (0, 0)),
        ],
        out_shape=[jax.ShapeDtypeStruct((128, 128, 128), BF)] * 2
        + [jax.ShapeDtypeStruct((64, 128), F32)],
        scratch_shapes=[pltpu.VMEM((4096, 128), BF), pltpu.VMEM((512, 128), BF)],
        compiler_params=pltpu.CompilerParams(vmem_limit_bytes=LIMIT),
        name="prep",
    )(count, rows, w)


def gather_kernel(x, g, ss, zs, ys, ks, ls):
    z, yl, k, col = place()
    up, down = lax.rem(z + 1, 8), lax.rem(z + 7, 8)

    def dev(zz, yy, kk):
        return (zz * 4 + yy * 2 + kk, col)

    along = (dev(up, yl, k), dev(down, yl, k))
    across, sibling = dev(z, 1 - yl, k), dev(z, yl, 1 - k)
    greet((*along, across, sibling))

    def at(zz, yy):
        return pl.multiple_of((zz * 4 + yy * 2 + k) * ND, ND)

    sent = []
    last = {}

    def send(src, base, lo, n, sem, target):
        cp = pltpu.make_async_remote_copy(
            src_ref=x.at[pl.ds(lo, n)] if src is x else g.at[pl.ds(base + lo, n)],
            dst_ref=g.at[pl.ds(base + lo, n)],
            send_sem=ss.at[len(sent)],
            recv_sem=sem,
            device_id=target,
            device_id_type=MESH,
        )
        cp.start()
        sent.append(cp)
        return cp

    to_sibling = []

    def share(src, base, lo, n):
        to_sibling.append(send(src, base, lo, n, ks.at[len(to_sibling)], sibling))

    own = at(z, yl)
    for part in range(2):
        lo = part * 256
        last["y", part] = send(x, own, lo, 256, ys.at[part], across)
        for d in range(2):
            last[d, 1, part] = send(x, own, lo, 256, zs.at[d, 0, part], along[d])
    share(x, own, 0, 512)
    mine = pltpu.make_async_copy(x, g.at[pl.ds(own, ND)], ls)
    mine.start()

    partner = at(z, 1 - yl)
    last["y", 0].wait_recv()
    for d in range(2):
        last[d, 1, 2] = send(g, partner, 0, 256, zs.at[d, 0, 2], along[d])
    share(g, partner, 0, 256)
    crossing = [(last["y", 1], partner)]
    for step in range(1, 5):
        arriving, crossing = crossing, []
        for part in range(3):
            for d in range(2):
                if (d, step, part) not in last:
                    continue
                zz = lax.rem(z + (8 - step if d == 0 else step), 8)
                base = at(zz, yl if part < 2 else 1 - yl)
                lo, n = (0, 256, 0)[part], 256
                if step == 4 and part == 2:
                    lo, n = d * 128, 128
                last[d, step, part].wait_recv()
                sem = zs.at[d, step, part] if step < 4 else None
                if step < 3:
                    last[d, step + 1, part] = send(g, base, lo, n, sem, along[d])
                elif step == 3 and part == d:
                    last[d, 4, part] = send(g, base, lo, n, sem, along[d])
                elif step == 3 and part == 2:
                    last[d, 4, part] = send(g, base, d * 128, 128, sem, along[d])
                if part == 1:
                    cp = send(g, base, 256, 256, ys.at[2 * step + d], across)
                    crossing.append((cp, at(zz, 1 - yl)))
                share(g, base, lo, n)
        for cp, base in arriving:
            cp.wait_recv()
            share(g, base, 256, 256)
    for cp, base in crossing:
        cp.wait_recv()
        share(g, base, 256, 256)
    for cp in to_sibling:
        cp.wait_recv()
    for cp in sent:
        cp.wait_send()
    mine.wait()


def gather_rows(x):
    return pl.pallas_call(
        gather_kernel,
        out_shape=jax.ShapeDtypeStruct((32 * ND, 128), BF),
        in_specs=[ANY],
        out_specs=ANY,
        scratch_shapes=[
            pltpu.SemaphoreType.DMA((80,)),
            pltpu.SemaphoreType.DMA((2, 4, 3)),
            pltpu.SemaphoreType.DMA((10,)),
            pltpu.SemaphoreType.DMA((40,)),
            pltpu.SemaphoreType.DMA,
        ],
        compiler_params=pltpu.CompilerParams(
            collective_id=0, has_side_effects=True, vmem_limit_bytes=LIMIT
        ),
        name="gather_rows",
    )(x)


def two_blocks(a, b):
    zero = jnp.zeros((64, 128), BF)
    return jnp.concatenate(
        [jnp.concatenate([a, zero], 1), jnp.concatenate([zero, b], 1)], 0
    )


def spread_kernel(near, far, cnt, frm, to, blocks, table, out, acc):
    acc[...] = jnp.zeros_like(acc)

    def block(ref, s):
        return pl.ds(pl.multiple_of(ref[s] * 64, 64), 64)

    @pl.loop(0, (cnt[0] + 4 * UNROLL - 1) // (4 * UNROLL))
    def _(i):
        parts = []
        for u in range(UNROLL):
            g = i * UNROLL + u
            for half in range(2):
                first = 4 * g + near * half
                second = first + far
                both = two_blocks(table[block(frm, first), :], table[block(frm, second), :])
                lhs = blocks[g, half * 64 : half * 64 + 64, :]
                prod = jnp.dot(lhs, both, preferred_element_type=F32)
                parts.append((first, prod[:, :128]))
                parts.append((second, prod[:, 128:]))
        for s, value in parts:
            acc[block(to, s), :] += value

    out[...] = acc[...].astype(BF)


def spread(near, far, n, count, frm, to, blocks, table, name):
    return pl.pallas_call(
        functools.partial(spread_kernel, near, far),
        out_shape=jax.ShapeDtypeStruct((n, 128), BF),
        in_specs=[SMEM, SMEM, SMEM, VMEM, VMEM],
        out_specs=VMEM,
        scratch_shapes=[pltpu.VMEM((n, 128), F32)],
        compiler_params=pltpu.CompilerParams(vmem_limit_bytes=LIMIT),
        name=name,
    )(count, frm, to, blocks, table)


def upright(rows, width):
    eye = lax.broadcasted_iota(jnp.int32, (width, 128), 0) == lax.broadcasted_iota(
        jnp.int32, (width, 128), 1
    )
    return jnp.concatenate(
        [
            jnp.sum(jnp.where(eye, rows[i : i + 1, :], 0.0), axis=1, keepdims=True)
            for i in range(rows.shape[0])
        ],
        0,
    )


def node_kernel(
    raw_part, deg, x, ws, wn, mask, cot,
    hidden, group, own_term, gsum,
    rb, rd, nat, sc, gg, rg, ss, s1, s2, s3, s4, ls,
):
    row, col = lax.axis_index("row"), lax.axis_index("col")
    peers = [lax.rem(col + o, 8) for o in range(8)]
    greet([(row, p) for p in peers[1:]])
    sent = []

    def send(src, dst, sem, o):
        cp = pltpu.make_async_remote_copy(
            src_ref=src,
            dst_ref=dst,
            send_sem=ss.at[len(sent)],
            recv_sem=sem,
            device_id=(row, peers[o]),
            device_id_type=MESH,
        )
        cp.start()
        sent.append(cp)
        return cp

    here = pltpu.make_async_copy(raw_part.at[pl.ds(pl.multiple_of(col * ND, ND), ND)], rb.at[0], ls.at[0])
    here.start()
    got = []
    for o in range(1, 8):
        j = peers[o]
        got.append(send(deg.at[pl.ds(pl.multiple_of(j * 8, 8), 8)], rd.at[o], s2.at[o], o))
        got.append(send(raw_part.at[pl.ds(pl.multiple_of(j * ND, ND), ND)], rb.at[o], s1.at[o], o))
    rd[0] = deg[pl.ds(pl.multiple_of(col * 8, 8), 8), :]
    feats = x[...]
    pre_self = jnp.dot(feats, ws[...], preferred_element_type=F32)
    keep = upright(mask[...].astype(F32), 128)
    here.wait()
    for cp in got:
        cp.wait_recv()
    degree = upright(jnp.sum(rd[...], axis=0), 64)
    raw = rb[0].astype(F32)
    for o in range(1, 8):
        raw = raw + rb[o].astype(F32)
    raw = raw.reshape(8, 2, 32, 128)
    for p in range(2):
        nat[pl.ds(p, 256, stride=2), :] = raw[:, p].reshape(256, 128)
    agg = (nat[...] / degree).astype(BF)
    pre = pre_self + jnp.dot(agg, wn[...], preferred_element_type=F32)
    sig = jax.nn.sigmoid(pre)
    dpre = (cot[...].astype(F32) * keep * sig * (1.0 + pre * (1.0 - sig))).astype(BF)
    nt = (((1,), (1,)), ((), ()))
    tn = (((0,), (0,)), ((), ()))
    nat[...] = lax.dot_general(dpre, wn[...], nt, preferred_element_type=F32) / degree
    for p in range(2):
        part = nat[pl.ds(p, 256, stride=2), :].astype(BF).reshape(8, 32, 128)
        for i in range(8):
            sc[i * 64 + p * 32 : i * 64 + p * 32 + 32, :] = part[i]
    mine = pl.ds(pl.multiple_of(col * ND, ND), ND)
    got = [send(sc, group.at[mine], s3.at[o], o) for o in range(1, 8)]
    stay = pltpu.make_async_copy(sc, group.at[mine], ls.at[1])
    stay.start()
    g_self = lax.dot_general(feats, dpre, tn, preferred_element_type=F32)
    g_neigh = lax.dot_general(agg, dpre, tn, preferred_element_type=F32)
    for i, value in enumerate((g_self[:, :128], g_self[:, 128:], g_neigh[:, :128], g_neigh[:, 128:])):
        gg[i * 128 : i * 128 + 128, :] = value
    grads = []
    for o in range(1, 8):
        j = pl.multiple_of(peers[o] * 64, 64)
        grads.append(send(gg.at[pl.ds(j, 64)], rg.at[o], s4.at[o], o))
    hidden[...] = (pre * sig).astype(BF)
    own_term[...] = lax.dot_general(dpre, ws[...], nt, preferred_element_type=F32)
    total = gg[pl.ds(pl.multiple_of(col * 64, 64), 64), :]
    for o in range(1, 8):
        grads[o - 1].wait_recv()
        total = total + rg[o]
    gsum[...] = total
    for cp in got:
        cp.wait_recv()
    stay.wait()
    for cp in sent:
        cp.wait_send()


def node(raw_part, deg, x, ws, wn, mask, cot):
    return pl.pallas_call(
        node_kernel,
        out_shape=[
            jax.ShapeDtypeStruct((ND, 256), BF),
            jax.ShapeDtypeStruct((8 * ND, 128), BF),
            jax.ShapeDtypeStruct((ND, 128), F32),
            jax.ShapeDtypeStruct((64, 128), F32),
        ],
        in_specs=[ANY, VMEM, VMEM, VMEM, VMEM, VMEM, VMEM],
        out_specs=[VMEM, ANY, VMEM, VMEM],
        scratch_shapes=[
            pltpu.VMEM((8, ND, 128), BF),
            pltpu.VMEM((8, 8, 128), F32),
            pltpu.VMEM((ND, 128), F32),
            pltpu.VMEM((ND, 128), BF),
            pltpu.VMEM((ND, 128), F32),
            pltpu.VMEM((8, 64, 128), F32),
            pltpu.SemaphoreType.DMA((28,)),
            pltpu.SemaphoreType.DMA((8,)),
            pltpu.SemaphoreType.DMA((8,)),
            pltpu.SemaphoreType.DMA((8,)),
            pltpu.SemaphoreType.DMA((8,)),
            pltpu.SemaphoreType.DMA((2,)),
        ],
        compiler_params=pltpu.CompilerParams(
            collective_id=1, has_side_effects=True, vmem_limit_bytes=LIMIT
        ),
        name="node",
    )(raw_part, deg, x, ws, wn, mask, cot)


def scatter_kernel(
    t, own_term, gpart,
    out, grad_self, grad_neigh,
    own, sib, ysrc, yb, zsrc, rz, fsrc, fy, gq, gz, gp, gsl, gall,
    ss, zs, ys, ks, ls, q1, q2, q3, q4,
):
    z, yl, k, col = place()

    def dev(zz, yy, kk, cc=None):
        return (zz * 4 + yy * 2 + kk, col if cc is None else cc)

    zat = [lax.rem(z + e, 8) for e in range(8)]
    cat = [lax.rem(col + o, 8) for o in range(8)]
    along = (dev(zat[7], yl, k), dev(zat[1], yl, k))
    across, sibling = dev(z, 1 - yl, k), dev(z, yl, 1 - k)
    quad = (sibling, across, dev(z, 1 - yl, 1 - k))
    greet(
        [*quad]
        + [dev(zat[e], yl, k) for e in range(1, 8)]
        + [dev(z, yl, k, cat[o]) for o in range(1, 8)]
    )
    sent = []

    def send(src, dst, sem, target):
        cp = pltpu.make_async_remote_copy(
            src_ref=src,
            dst_ref=dst,
            send_sem=ss.at[len(sent)],
            recv_sem=sem,
            device_id=target,
            device_id_type=MESH,
        )
        cp.start()
        sent.append(cp)
        return cp

    loads, sibs = {}, {}
    order = (4, 3, 5, 2, 6, 1, 7, 0)
    for e in order:
        for r in (1, 0):
            yy = yl if r == 0 else 1 - yl
            base = (zat[e] * 4 + yy * 2) * ND
            theirs = pl.ds(pl.multiple_of(base + (1 - k) * ND, ND), ND)
            ours = pl.ds(pl.multiple_of(base + k * ND, ND), ND)
            sibs[e, r] = send(t.at[theirs], sib.at[e, r], ks.at[e, r], sibling)
            loads[e, r] = pltpu.make_async_copy(t.at[ours], own.at[e, r], ls.at[e, r])
            loads[e, r].start()
    quads = [send(gpart, gq.at[i], q1.at[i], quad[i]) for i in range(3)]

    ready = set()

    def mine(e, r, lo, n):
        if (e, r) not in ready:
            loads[e, r].wait()
            sibs[e, r].wait_recv()
            ready.add((e, r))
        return own[e, r, lo : lo + n, :].astype(F32) + sib[e, r, lo : lo + n, :].astype(F32)

    ysent = {}

    def cross(e):
        ysrc[e] = mine(e, 1, 256, 256).astype(BF)
        ysent[e] = send(ysrc.at[e], yb.at[e], ys.at[e], across)

    crossed = set()

    def base_value(e, part, lo, n):
        if part == 2:
            return mine(e, 1, lo, n)
        if part == 0:
            return mine(e, 0, lo, n)
        if e not in crossed:
            ysent[e].wait_recv()
            crossed.add(e)
        return mine(e, 0, 256 + lo, n) + yb[e, lo : lo + n, :].astype(F32)

    zsent = {}

    def piece(d, step, part):
        e = (8 - step) % 8 if d == 0 else step
        lo, n = (0, 256) if (step < 4 or part < 2) else (d * 128, 128)
        value = base_value(e, part, lo, n)
        if step < 3 or (step == 3 and part == d):
            zsent[d, step + 1, part].wait_recv()
            value = value + rz[d, step, part * 256 : part * 256 + 256, :].astype(F32)
        elif step == 3 and part == 2:
            zsent[d, 4, 2].wait_recv()
            more = rz[d, 3, 512 + d * 128 : 640 + d * 128, :].astype(F32)
            halves = [value[:128], value[128:]]
            halves[d] = halves[d] + more
            value = jnp.concatenate(halves, 0)
        at = pl.ds(part * 256 + lo, n)
        zsrc[d, step - 1, at, :] = value.astype(BF)
        zsent[d, step, part] = send(
            zsrc.at[d, step - 1, at], rz.at[d, step - 1, at], zs.at[d, step - 1, part], along[d]
        )

    cross(4)
    piece(0, 4, 2)
    piece(1, 4, 2)
    piece(0, 4, 0)
    cross(3)
    cross(5)
    piece(1, 4, 1)
    cross(2)
    cross(6)
    cross(1)
    cross(7)
    cross(0)
    total = gpart[...]
    for i in range(3):
        quads[i].wait_recv()
        total = total + gq[i]
    gz[...] = total
    zred = {}
    for e in range(1, 8):
        src = gz.at[pl.ds(pl.multiple_of(zat[e] * 8, 8), 8)]
        zred[e] = send(src, gp.at[e], q2.at[e], dev(zat[e], yl, k))
    for part in (2, 0, 1):
        for d in range(2):
            piece(d, 3, part)
    here = pl.ds(pl.multiple_of(z * 8, 8), 8)
    gp[0] = gz[here, :]
    for e in range(1, 8):
        zred[e].wait_recv()
    gsl[here, :] = jnp.sum(gp[...], axis=0)
    zall = [send(gsl.at[here], gsl.at[here], q3.at[e], dev(zat[e], yl, k)) for e in range(1, 8)]
    for part in (2, 0, 1):
        for d in range(2):
            piece(d, 2, part)
    for cp in zall:
        cp.wait_recv()
    slot = pl.ds(pl.multiple_of(col * 64, 64), 64)
    gall[slot, :] = gsl[...]
    call = [send(gsl, gall.at[slot], q4.at[o], dev(z, yl, k, cat[o])) for o in range(1, 8)]
    for part in (2, 0, 1):
        for d in range(2):
            piece(d, 1, part)

    def final(part):
        value = base_value(0, part, 0, 256)
        for d in range(2):
            zsent[d, 1, part].wait_recv()
            value = value + rz[d, 0, part * 256 : part * 256 + 256, :].astype(F32)
        return value

    fsrc[...] = final(2).astype(BF)
    last = send(fsrc, fy, ys.at[8], across)
    for cp in call:
        cp.wait_recv()
    grad_self[:, :128] = gall[:128, :]
    grad_self[:, 128:] = gall[128:256, :]
    grad_neigh[:, :128] = gall[256:384, :]
    grad_neigh[:, 128:] = gall[384:, :]
    first = final(0) + own_term[:256, :]
    out[256:, :] = (final(1) + own_term[256:, :]).astype(BF)
    last.wait_recv()
    out[:256, :] = (first + fy[...].astype(F32)).astype(BF)
    for cp in sent:
        cp.wait_send()


def scatter_rows(t, own_term, gpart):
    return pl.pallas_call(
        scatter_kernel,
        out_shape=[
            jax.ShapeDtypeStruct((ND, 128), BF),
            jax.ShapeDtypeStruct((128, 256), F32),
            jax.ShapeDtypeStruct((128, 256), F32),
        ],
        in_specs=[ANY, VMEM, VMEM],
        out_specs=[VMEM, VMEM, VMEM],
        scratch_shapes=[
            pltpu.VMEM((8, 2, ND, 128), BF),
            pltpu.VMEM((8, 2, ND, 128), BF),
            pltpu.VMEM((8, 256, 128), BF),
            pltpu.VMEM((8, 256, 128), BF),
            pltpu.VMEM((2, 4, 768, 128), BF),
            pltpu.VMEM((2, 4, 768, 128), BF),
            pltpu.VMEM((256, 128), BF),
            pltpu.VMEM((256, 128), BF),
            pltpu.VMEM((3, 64, 128), F32),
            pltpu.VMEM((64, 128), F32),
            pltpu.VMEM((8, 8, 128), F32),
            pltpu.VMEM((64, 128), F32),
            pltpu.VMEM((512, 128), F32),
            pltpu.SemaphoreType.DMA((80,)),
            pltpu.SemaphoreType.DMA((2, 4, 3)),
            pltpu.SemaphoreType.DMA((9,)),
            pltpu.SemaphoreType.DMA((8, 2)),
            pltpu.SemaphoreType.DMA((8, 2)),
            pltpu.SemaphoreType.DMA((3,)),
            pltpu.SemaphoreType.DMA((8,)),
            pltpu.SemaphoreType.DMA((8,)),
            pltpu.SemaphoreType.DMA((8,)),
        ],
        compiler_params=pltpu.CompilerParams(
            collective_id=2, has_side_effects=True, vmem_limit_bytes=LIMIT
        ),
        name="scatter_rows",
    )(t, own_term, gpart)


def shards(
    features,
    self_weight,
    neigh_weight,
    block_row,
    block_col,
    block_count,
    edge_weight,
    train_mask,
    out_cotangent,
):
    rows = block_row.reshape(512)
    cols = block_col.reshape(512)
    count = block_count.reshape(1)
    mask = train_mask.reshape(4, 128)
    zf, zt, deg = prep(count, block_row.reshape(1, 512), edge_weight.reshape(512, 4096))
    gathered = gather_rows(features)
    raw_part = spread(1, 2, 8 * ND, count, cols, rows, zf, gathered, "forward")
    hidden, group, own_term, gsum = node(
        raw_part, deg, features, self_weight, neigh_weight, mask, out_cotangent
    )
    through = spread(2, 1, 32 * ND, count, rows, cols, zt, group, "backward")
    grad_input, grad_self, grad_neigh = scatter_rows(through, own_term, gsum)
    return hidden, grad_input, grad_self, grad_neigh


def solution(mesh):
    in_specs = (
        P(("row", "col"), None),
        P(),
        P(),
        P("row", "col", None),
        P("row", "col", None),
        P("row", "col"),
        P("row", "col", None, None),
        P(("row", "col")),
        P(("row", "col"), None),
    )
    out_specs = (P(("row", "col"), None), P(("row", "col"), None), P(), P())
    return jax.shard_map(shards, mesh=mesh, in_specs=in_specs, out_specs=out_specs, check_vma=False)
```

```python
import functools

import jax
import jax.numpy as jnp
from jax import lax
from jax.experimental import pallas as pl
from jax.experimental.pallas import tpu as pltpu
from jax.sharding import PartitionSpec as P

MESH = pl.DeviceIdType.MESH
BF = jnp.bfloat16
F32 = jnp.float32
VMEM = pl.BlockSpec(memory_space=pltpu.VMEM)
SMEM = pl.BlockSpec(memory_space=pltpu.SMEM)
ANY = pl.BlockSpec(memory_space=pl.ANY)
ND = 512
UNROLL = 16
WORK = (8, 3, 3, 2, 2)
TURN = (32, 32, 24)


def place():
    row = lax.axis_index("row")
    return row // 4, (row // 2) % 2, row % 2, lax.axis_index("col")


def greet(targets):
    barrier = pltpu.get_barrier_semaphore()
    for target in targets:
        pl.semaphore_signal(barrier, inc=1, device_id=target, device_id_type=MESH)
    pl.semaphore_wait(barrier, len(targets))


def sender(ss):
    sent = []

    def send(src, dst, sem, target):
        cp = pltpu.make_async_remote_copy(
            src_ref=src,
            dst_ref=dst,
            send_sem=ss.at[len(sent)],
            recv_sem=sem,
            device_id=target,
            device_id_type=MESH,
        )
        cp.start()
        sent.append(cp)
        return cp

    return send, sent


def ring_gather(half, x, table, base, send, zs, ys, along, across, share, idle):
    last = {}

    def go(src, row, lo, n, sem, target):
        return send(
            x.at[pl.ds(lo, n)] if src is x else table.at[pl.ds(row + lo, n)],
            table.at[pl.ds(row + lo, n)],
            sem,
            target,
        )

    own, partner = base(0, 0), base(0, 1)
    first = go(x, own, 0, 256, ys.at[0], across)
    for part in (1, 0):
        for d in range(2):
            last[d, 1, part] = go(x, own, part * 256, 256, zs.at[d, 0, part], along[d])
    crossing = [(go(x, own, 256, 256, ys.at[1], across), partner)]
    share(x, own, 0, 512)
    idle(0)
    first.wait_recv()
    for d in range(2):
        last[d, 1, 2] = go(table, partner, 0, 256, zs.at[d, 0, 2], along[d])
    share(table, partner, 0, 256)
    for step in range(1, half + 1):
        arriving, crossing = crossing, []
        for part in (1, 2, 0):
            for d in range(2):
                if (d, step, part) not in last:
                    continue
                e = 2 * half - step if d == 0 else step
                row = base(e, 0 if part < 2 else 1)
                lo, n = (0, 256, 0)[part], 256
                if step == half and part == 2:
                    lo, n = d * 128, 128
                last[d, step, part].wait_recv()
                if step < half - 1 or (step == half - 1 and part == d):
                    last[d, step + 1, part] = go(table, row, lo, n, zs.at[d, step, part], along[d])
                elif step == half - 1 and part == 2:
                    last[d, half, 2] = go(table, row, d * 128, 128, zs.at[d, step, 2], along[d])
                if part == 1:
                    cp = go(table, row, 256, 256, ys.at[2 * step + d], across)
                    crossing.append((cp, base(e, 1)))
                share(table, row, lo, n)
                idle(step)
        for cp, row in arriving:
            cp.wait_recv()
            share(table, row, 256, 256)
    for cp, row in crossing:
        cp.wait_recv()
        share(table, row, 256, 256)


def ring_reduce(half, value, direct, zsrc, rz, send, zs, along):
    zsent = {}

    def arrived(d, step, part, lo, n):
        return rz[d, step, part * 256 + lo : part * 256 + lo + n, :].astype(F32)

    def piece(d, step, part):
        e = (2 * half - step) if d == 0 else step
        lo, n = (0, 256) if (step < half or part < 2) else (d * 128, 128)
        at = pl.ds(part * 256 + lo, n)
        alone = step == half or (step == half - 1 and part == 1 - d)
        src = direct(e, part, lo, n) if alone else None
        if src is None:
            total = value(e, part, lo, n)
            if step < half - 1 or (step == half - 1 and part == d):
                zsent[d, step + 1, part].wait_recv()
                total = total + arrived(d, step, part, 0, 256)
            elif step == half - 1 and part == 2:
                zsent[d, half, 2].wait_recv()
                halves = [total[:128], total[128:]]
                halves[d] = halves[d] + arrived(d, step, 2, d * 128, 128)
                total = jnp.concatenate(halves, 0)
            zsrc[d, step - 1, at, :] = total.astype(BF)
            src = zsrc.at[d, step - 1, at]
        zsent[d, step, part] = send(src, rz.at[d, step - 1, at], zs.at[d, step - 1, part], along[d])

    def final(part):
        total = value(0, part, 0, 256)
        for d in range(2):
            zsent[d, 1, part].wait_recv()
            total = total + arrived(d, 0, part, 0, 256)
        return total

    return piece, final


def gather_kernel(
    cnt, rows, x, w,
    g, zf, deg,
    wv, pat, dsl, ss, zs, ys, ks, ls, wsem,
):
    z, yl, k, col = place()

    def dev(zz, yy, kk):
        return (zz * 4 + yy * 2 + kk, col)

    slabs = []
    for i in range(8):
        slabs.append(pltpu.make_async_copy(w.at[pl.ds(i * 64, 64)], wv.at[pl.ds(i * 64, 64)], wsem.at[i]))
        slabs[-1].start()
    along = (dev(lax.rem(z + 1, 8), yl, k), dev(lax.rem(z + 7, 8), yl, k))
    across, sibling = dev(z, 1 - yl, k), dev(z, yl, 1 - k)
    greet((*along, across, sibling))
    send, sent = sender(ss)

    def base(e, r):
        yy = yl if r == 0 else 1 - yl
        return pl.multiple_of((lax.rem(z + e, 8) * 4 + yy * 2 + k) * ND, ND)

    to_sibling = []

    def share(src, row, lo, n):
        at = pl.ds(row + lo, n)
        src = x.at[pl.ds(lo, n)] if src is x else g.at[at]
        to_sibling.append(send(src, g.at[at], ks.at[len(to_sibling)], sibling))

    low = lax.broadcasted_iota(jnp.int32, (32, 128), 1) < 64
    lim = cnt[0]
    done = [0]

    def unit(i):
        b = pl.multiple_of(i * 8, 8)
        live = (b + lax.broadcasted_iota(jnp.int32, (8, 4096), 0)) < lim
        y = jnp.where(live, wv[pl.ds(b, 8), :], 0).astype(F32).reshape(8, 32, 128)
        for h4 in range(2):
            y4 = [y[h4 * 4 + s] for s in range(4)]
            r4 = [pltpu.roll(v, 64, 1) for v in y4]
            zf[i * 2 + h4] = jnp.concatenate(
                [
                    jnp.where(low, y4[0], r4[2]),
                    jnp.where(low, r4[0], y4[2]),
                    jnp.where(low, y4[1], r4[3]),
                    jnp.where(low, r4[1], y4[3]),
                ],
                0,
            ).astype(BF)

    def work(n):
        n = min(n, 64 - done[0])
        if n <= 0:
            return
        lo = done[0]
        for i in range(lo // 8 if lo % 8 == 0 else lo // 8 + 1, (lo + n - 1) // 8 + 1):
            slabs[i].wait()
        pl.loop(lo, lo + n)(unit)
        for i in range(lo // 8, (lo + n) // 8):
            at = pl.ds(i * 64, 64)
            dsl[at, :] = jnp.dot(
                wv[at, :].astype(F32).astype(BF), pat[...], preferred_element_type=F32
            ).astype(BF)
        done[0] += n

    def idle(step):
        work(WORK[step])

    def prepare(step):
        if step == 0:
            at = lax.broadcasted_iota(jnp.int32, (4096, 128), 0) // 64
            pat[...] = (at == lax.broadcasted_iota(jnp.int32, (4096, 128), 1)).astype(BF)
        idle(step)

    mine = pltpu.make_async_copy(x, g.at[pl.ds(base(0, 0), ND)], ls)
    mine.start()
    ring_gather(4, x, g, base, send, zs, ys, along, across, share, prepare)
    work(64)
    slot = lax.broadcasted_iota(jnp.int32, (64, 512), 1)
    hot = (lax.broadcasted_iota(jnp.int32, (64, 512), 0) == rows[...]) & (slot < lim)
    deg[...] = jnp.dot(hot.astype(F32).astype(BF), dsl[...], preferred_element_type=F32)
    for cp in to_sibling:
        cp.wait_recv()
    for cp in sent:
        cp.wait_send()
    mine.wait()


def gather_rows(count, rows, x, w):
    return pl.pallas_call(
        gather_kernel,
        out_shape=[
            jax.ShapeDtypeStruct((32 * ND, 128), BF),
            jax.ShapeDtypeStruct((128, 128, 128), BF),
            jax.ShapeDtypeStruct((64, 128), F32),
        ],
        in_specs=[SMEM, VMEM, ANY, pl.BlockSpec(memory_space=pltpu.HBM)],
        out_specs=[ANY, VMEM, VMEM],
        scratch_shapes=[
            pltpu.VMEM((512, 4096), jnp.int32),
            pltpu.VMEM((4096, 128), BF),
            pltpu.VMEM((512, 128), BF),
            pltpu.SemaphoreType.DMA((80,)),
            pltpu.SemaphoreType.DMA((2, 4, 3)),
            pltpu.SemaphoreType.DMA((10,)),
            pltpu.SemaphoreType.DMA((40,)),
            pltpu.SemaphoreType.DMA,
            pltpu.SemaphoreType.DMA((8,)),
        ],
        compiler_params=pltpu.CompilerParams(
            collective_id=0, has_side_effects=True, vmem_limit_bytes=43 << 20
        ),
        name="gather_rows",
    )(count, rows, x, w)


def two_blocks(a, b):
    zero = jnp.zeros((64, 128), BF)
    return jnp.concatenate(
        [jnp.concatenate([a, zero], 1), jnp.concatenate([zero, b], 1)], 0
    )


def spread_kernel(near, far, cnt, frm, to, blocks, table, out, acc):
    acc[...] = jnp.zeros_like(acc)

    def block(ref, s):
        return pl.ds(pl.multiple_of(ref[s] * 64, 64), 64)

    @pl.loop(0, (cnt[0] + 4 * UNROLL - 1) // (4 * UNROLL))
    def _(i):
        parts = []
        for u in range(UNROLL):
            g = i * UNROLL + u
            for half in range(2):
                first = 4 * g + near * half
                second = first + far
                both = two_blocks(table[block(frm, first), :], table[block(frm, second), :])
                lhs = blocks[g, half * 64 : half * 64 + 64, :]
                prod = jnp.dot(lhs, both, preferred_element_type=F32)
                parts.append((first, prod[:, :128]))
                parts.append((second, prod[:, 128:]))
        for s, value in parts:
            acc[block(to, s), :] += value

    out[...] = acc[...].astype(BF)


def forward(count, frm, to, blocks, table):
    return pl.pallas_call(
        functools.partial(spread_kernel, 1, 2),
        out_shape=jax.ShapeDtypeStruct((8 * ND, 128), BF),
        in_specs=[SMEM, SMEM, SMEM, VMEM, VMEM],
        out_specs=VMEM,
        scratch_shapes=[pltpu.VMEM((8 * ND, 128), F32)],
        compiler_params=pltpu.CompilerParams(vmem_limit_bytes=16 << 20),
        name="forward",
    )(count, frm, to, blocks, table)


def backward_kernel(cnt, frm, to, blocks, table, hidden, out, kept, acc, sem):
    keep = pltpu.make_async_copy(hidden, kept, sem)
    keep.start()
    spread_kernel(2, 1, cnt, frm, to, blocks, table, out, acc)
    keep.wait()


def backward(count, frm, to, blocks, table, hidden):
    return pl.pallas_call(
        backward_kernel,
        out_shape=[
            jax.ShapeDtypeStruct((32 * ND, 128), BF),
            jax.ShapeDtypeStruct(hidden.shape, hidden.dtype),
        ],
        in_specs=[SMEM, SMEM, SMEM, VMEM, VMEM, ANY],
        out_specs=[VMEM, ANY],
        scratch_shapes=[pltpu.VMEM((32 * ND, 128), F32), pltpu.SemaphoreType.DMA],
        compiler_params=pltpu.CompilerParams(vmem_limit_bytes=20 << 20),
        name="backward",
    )(count, frm, to, blocks, table, hidden)


def upright(rows, width):
    eye = lax.broadcasted_iota(jnp.int32, (width, 128), 0) == lax.broadcasted_iota(
        jnp.int32, (width, 128), 1
    )
    return jnp.concatenate(
        [
            jnp.sum(jnp.where(eye, rows[i : i + 1, :], 0.0), axis=1, keepdims=True)
            for i in range(rows.shape[0])
        ],
        0,
    )


def node_kernel(
    raw_part, deg, x, ws, wn, mask, cot, zf,
    hidden, group, own_term, gsum, zt,
    yb, zsrc, rz, fsrc, fy, rd, nat, sc, grads, gr, ss, z1, y1, z2, y2, ds, gsem, ls,
):
    row, col = lax.axis_index("row"), lax.axis_index("col")
    yh, xx = col // 4, lax.rem(col, 4)
    z, side = row // 4, lax.rem(row, 4)
    zat = [lax.rem(z + e, 8) for e in range(8)]
    xat = [lax.rem(xx + e, 4) for e in range(4)]
    peers = [lax.rem(col + o, 8) for o in range(8)]
    up, down = (row, yh * 4 + xat[1]), (row, yh * 4 + xat[3])
    across = (row, (1 - yh) * 4 + xx)
    greet([(row, p) for p in peers[1:]] + [(zat[e] * 4 + side, col) for e in range(1, 8)])
    send, sent = sender(ss)

    def base(e, r):
        return pl.multiple_of(((yh if r == 0 else 1 - yh) * 4 + xat[e]) * ND, ND)

    def part_ref(e, part, lo, n):
        row0 = base(e, 1 if part == 2 else 0) + (256 if part == 1 else 0)
        return raw_part.at[pl.ds(row0 + lo, n)]

    ysent = {}

    def cross(e):
        ysent[e] = send(raw_part.at[pl.ds(base(e, 1) + 256, 256)], yb.at[e], y1.at[e], across)

    crossed = set()

    def value(e, part, lo, n):
        total = part_ref(e, part, lo, n)[...].astype(F32)
        if part == 1:
            if e not in crossed:
                ysent[e].wait_recv()
                crossed.add(e)
            total = total + yb[e, lo : lo + n, :].astype(F32)
        return total

    def direct(e, part, lo, n):
        return None if part == 1 else part_ref(e, part, lo, n)

    piece, final = ring_reduce(2, value, direct, zsrc, rz, send, z1, (down, up))

    def turn(lo, n):
        @pl.loop(lo, lo + n)
        def _(i):
            zt[i] = zf[i].T

    cross(2)
    piece(0, 2, 2)
    piece(1, 2, 2)
    piece(0, 2, 0)
    cross(1)
    cross(3)
    piece(1, 1, 0)
    cross(0)
    rd[0] = deg[pl.ds(pl.multiple_of(col * 8, 8), 8), :]
    degs = []
    for o in range(1, 8):
        src = deg.at[pl.ds(pl.multiple_of(peers[o] * 8, 8), 8)]
        degs.append(send(src, rd.at[o], ds.at[o], (row, peers[o])))
    feats = x[...]
    pre_self = jnp.dot(feats, ws[...], preferred_element_type=F32)
    keep = upright(mask[...].astype(F32), 128)
    turn(0, TURN[0])
    piece(1, 2, 1)
    piece(0, 1, 1)
    piece(0, 1, 2)
    piece(1, 1, 2)
    piece(0, 1, 0)
    piece(1, 1, 1)
    for cp in degs:
        cp.wait_recv()
    degree = upright(jnp.sum(rd[...], axis=0), 64)
    turn(TURN[0], TURN[1])
    fsrc[...] = final(2).astype(BF)
    last = send(fsrc, fy, y1.at[4], across)
    second = final(1)
    first = final(0)
    turn(TURN[0] + TURN[1], TURN[2])
    last.wait_recv()
    raw = jnp.concatenate([first + fy[...].astype(F32), second], 0).reshape(8, 2, 32, 128)
    for p in range(2):
        nat[pl.ds(p, 256, stride=2), :] = raw[:, p].reshape(256, 128)
    agg = (nat[...] / degree).astype(BF)
    pre = pre_self + jnp.dot(agg, wn[...], preferred_element_type=F32)
    sig = jax.nn.sigmoid(pre)
    dpre = (cot[...].astype(F32) * keep * sig * (1.0 + pre * (1.0 - sig))).astype(BF)
    nt = (((1,), (1,)), ((), ()))
    tn = (((0,), (0,)), ((), ()))
    nat[...] = lax.dot_general(dpre, wn[...], nt, preferred_element_type=F32) / degree
    for p in range(2):
        part = nat[pl.ds(p, 256, stride=2), :].astype(BF).reshape(8, 32, 128)
        for i in range(8):
            sc[i * 64 + p * 32 : i * 64 + p * 32 + 32, :] = part[i]
    stay = pltpu.make_async_copy(sc, group.at[pl.ds(base(0, 0), ND)], ls)
    stay.start()
    todo = []
    slices = []

    def later():
        hidden[...] = (pre * sig).astype(BF)
        own_term[...] = lax.dot_general(dpre, ws[...], nt, preferred_element_type=F32)
        g_self = lax.dot_general(feats, dpre, tn, preferred_element_type=F32)
        g_neigh = lax.dot_general(agg, dpre, tn, preferred_element_type=F32)
        for i, v in enumerate((g_self[:, :128], g_self[:, 128:], g_neigh[:, :128], g_neigh[:, 128:])):
            grads[i * 128 : i * 128 + 128, :] = v
        for e in range(1, 8):
            src = grads.at[pl.ds(pl.multiple_of(zat[e] * 64, 64), 64)]
            slices.append(send(src, gr.at[e], gsem.at[e], (zat[e] * 4 + side, col)))

    def idle(step):
        if step == 0:
            later()
        elif not todo:
            todo.append(1)
            turn(sum(TURN[:3]), 128 - sum(TURN[:3]))

    ring_gather(
        2, sc, group, base, send, z2, y2, (up, down), across, lambda *a: None, idle
    )
    total = grads[pl.ds(pl.multiple_of(z * 64, 64), 64), :]
    for e in range(1, 8):
        slices[e - 1].wait_recv()
        total = total + gr[e]
    gsum[...] = total
    stay.wait()
    for cp in sent:
        cp.wait_send()


def node(raw_part, deg, x, ws, wn, mask, cot, zf):
    return pl.pallas_call(
        node_kernel,
        out_shape=[
            jax.ShapeDtypeStruct((ND, 256), BF),
            jax.ShapeDtypeStruct((8 * ND, 128), BF),
            jax.ShapeDtypeStruct((ND, 128), F32),
            jax.ShapeDtypeStruct((64, 128), F32),
            jax.ShapeDtypeStruct((128, 128, 128), BF),
        ],
        in_specs=[VMEM] * 8,
        out_specs=[VMEM, ANY, VMEM, VMEM, VMEM],
        scratch_shapes=[
            pltpu.VMEM((4, 256, 128), BF),
            pltpu.VMEM((2, 2, 768, 128), BF),
            pltpu.VMEM((2, 2, 768, 128), BF),
            pltpu.VMEM((256, 128), BF),
            pltpu.VMEM((256, 128), BF),
            pltpu.VMEM((8, 8, 128), F32),
            pltpu.VMEM((ND, 128), F32),
            pltpu.VMEM((ND, 128), BF),
            pltpu.VMEM((512, 128), F32),
            pltpu.VMEM((8, 64, 128), F32),
            pltpu.SemaphoreType.DMA((60,)),
            pltpu.SemaphoreType.DMA((2, 2, 3)),
            pltpu.SemaphoreType.DMA((5,)),
            pltpu.SemaphoreType.DMA((2, 2, 3)),
            pltpu.SemaphoreType.DMA((6,)),
            pltpu.SemaphoreType.DMA((8,)),
            pltpu.SemaphoreType.DMA((8,)),
            pltpu.SemaphoreType.DMA,
        ],
        compiler_params=pltpu.CompilerParams(
            collective_id=1, has_side_effects=True, vmem_limit_bytes=20 << 20
        ),
        name="node",
    )(raw_part, deg, x, ws, wn, mask, cot, zf)


def in_order(parts, me, n):
    total = None
    for p in range(n):
        i = lax.rem(me - p - 1 + 2 * n, n)
        total = parts[i] if total is None else total + parts[i]
    return total


def scatter_kernel(
    t, own_term, gpart,
    out, grad_self, grad_neigh,
    own, sib, ysrc, yb, zsrc, rz, fsrc, fy, gk, gx, gy, gsrc, gall,
    ss, zs, ys, ks, ls, q0, q1, q2, q3,
):
    z, yl, k, col = place()

    def dev(zz, yy, kk, cc=None):
        return (zz * 4 + yy * 2 + kk, col if cc is None else cc)

    zat = [lax.rem(z + e, 8) for e in range(8)]
    yh, xx = col // 4, lax.rem(col, 4)
    along = (dev(zat[7], yl, k), dev(zat[1], yl, k))
    across, sibling = dev(z, 1 - yl, k), dev(z, yl, 1 - k)
    far = (1 - yh) * 4 + xx
    ypeers = (across, dev(z, yl, k, far), dev(z, 1 - yl, k, far))
    xpeers = [dev(z, yl, k, yh * 4 + lax.rem(xx + e, 4)) for e in (1, 2, 3)]
    zpeers = [dev(zat[e], yl, k) for e in range(1, 8)]
    greet([sibling, *ypeers, *xpeers, *zpeers])
    send, sent = sender(ss)
    theirs = pl.ds(pl.multiple_of((1 - k) * 32, 32), 32)
    ours = pl.ds(pl.multiple_of(k * 32, 32), 32)
    halves = send(gpart.at[theirs], gk, q0.at[0], sibling)

    loads, sibs = {}, {}
    for e in (4, 3, 5, 2, 6, 1, 7, 0):
        for r in (1, 0):
            yy = yl if r == 0 else 1 - yl
            row = (zat[e] * 4 + yy * 2) * ND
            theirs = pl.ds(pl.multiple_of(row + (1 - k) * ND, ND), ND)
            ours = pl.ds(pl.multiple_of(row + k * ND, ND), ND)
            sibs[e, r] = send(t.at[theirs], sib.at[e, r], ks.at[e, r], sibling)
            loads[e, r] = pltpu.make_async_copy(t.at[ours], own.at[e, r], ls.at[e, r])
            loads[e, r].start()
    ready = set()

    def mine(e, r, lo, n):
        if (e, r) not in ready:
            loads[e, r].wait()
            sibs[e, r].wait_recv()
            ready.add((e, r))
        return own[e, r, lo : lo + n, :].astype(F32) + sib[e, r, lo : lo + n, :].astype(F32)

    ysent = {}

    def cross(e):
        ysrc[e] = mine(e, 1, 256, 256).astype(BF)
        ysent[e] = send(ysrc.at[e], yb.at[e], ys.at[e], across)

    crossed = set()

    def value(e, part, lo, n):
        if part == 2:
            return mine(e, 1, lo, n)
        if part == 0:
            return mine(e, 0, lo, n)
        if e not in crossed:
            ysent[e].wait_recv()
            crossed.add(e)
        return mine(e, 0, 256 + lo, n) + yb[e, lo : lo + n, :].astype(F32)

    piece, final = ring_reduce(4, value, lambda *a: None, zsrc, rz, send, zs, along)

    cross(4)
    piece(0, 4, 2)
    piece(1, 4, 2)
    piece(0, 4, 0)
    cross(3)
    cross(5)
    piece(1, 4, 1)
    cross(2)
    cross(6)
    cross(1)
    cross(7)
    cross(0)
    halves.wait_recv()
    total = gpart[pl.ds(pl.multiple_of(k * 32, 32), 32), :] + gk[...]
    gsrc[0] = total
    swaps = [send(gsrc.at[0], gx.at[i], q1.at[i], xpeers[i]) for i in range(3)]
    for part in (2, 0, 1):
        for d in range(2):
            piece(d, 3, part)
    gx[3] = gsrc[0]
    for cp in swaps:
        cp.wait_recv()
    total = in_order(gx, xx, 4)
    gsrc[1] = total
    swaps = [send(gsrc.at[1], gy.at[i], q2.at[i], ypeers[i]) for i in range(3)]
    for part in (2, 0, 1):
        for d in range(2):
            piece(d, 2, part)
    for cp in swaps:
        cp.wait_recv()
    total = (gsrc[1] + gy[0]) + (gy[1] + gy[2])
    mine_at = gall.at[z, k]
    gall[z, k] = total
    swaps = [send(mine_at, mine_at, q3.at[i], zpeers[i]) for i in range(7)]
    for part in (2, 0, 1):
        for d in range(2):
            piece(d, 1, part)
    fsrc[...] = final(2).astype(BF)
    last = send(fsrc, fy, ys.at[8], across)
    first = final(0) + own_term[:256, :]
    out[256:, :] = (final(1) + own_term[256:, :]).astype(BF)
    for cp in swaps:
        cp.wait_recv()
    other = send(gall.at[:, k], gall.at[:, k], q0.at[1], sibling)
    last.wait_recv()
    out[:256, :] = (first + fy[...].astype(F32)).astype(BF)
    other.wait_recv()
    for i, ref in enumerate((grad_self, grad_neigh)):
        for h in range(2):
            lo = i * 4 + h * 2
            ref[:, h * 128 : h * 128 + 128] = gall[lo : lo + 2].reshape(128, 128)
    for cp in sent:
        cp.wait_send()


def scatter_rows(t, own_term, grads):
    return pl.pallas_call(
        scatter_kernel,
        out_shape=[
            jax.ShapeDtypeStruct((ND, 128), BF),
            jax.ShapeDtypeStruct((128, 256), F32),
            jax.ShapeDtypeStruct((128, 256), F32),
        ],
        in_specs=[ANY, VMEM, VMEM],
        out_specs=[VMEM, VMEM, VMEM],
        scratch_shapes=[
            pltpu.VMEM((8, 2, ND, 128), BF),
            pltpu.VMEM((8, 2, ND, 128), BF),
            pltpu.VMEM((8, 256, 128), BF),
            pltpu.VMEM((8, 256, 128), BF),
            pltpu.VMEM((2, 4, 768, 128), BF),
            pltpu.VMEM((2, 4, 768, 128), BF),
            pltpu.VMEM((256, 128), BF),
            pltpu.VMEM((256, 128), BF),
            pltpu.VMEM((32, 128), F32),
            pltpu.VMEM((4, 32, 128), F32),
            pltpu.VMEM((3, 32, 128), F32),
            pltpu.VMEM((2, 32, 128), F32),
            pltpu.VMEM((8, 2, 32, 128), F32),
            pltpu.SemaphoreType.DMA((90,)),
            pltpu.SemaphoreType.DMA((2, 4, 3)),
            pltpu.SemaphoreType.DMA((9,)),
            pltpu.SemaphoreType.DMA((8, 2)),
            pltpu.SemaphoreType.DMA((8, 2)),
            pltpu.SemaphoreType.DMA((2,)),
            pltpu.SemaphoreType.DMA((3,)),
            pltpu.SemaphoreType.DMA((3,)),
            pltpu.SemaphoreType.DMA((7,)),
        ],
        compiler_params=pltpu.CompilerParams(
            collective_id=2, has_side_effects=True, vmem_limit_bytes=20 << 20
        ),
        name="scatter_rows",
    )(t, own_term, grads)


def finish_kernel(*refs):
    n = len(refs) // 2
    sem = refs[-1]
    copies = [pltpu.make_async_copy(refs[i], refs[n + i], sem.at[i]) for i in range(n)]
    for cp in copies:
        cp.start()
    for cp in copies:
        cp.wait()


def finish(*arrays):
    return pl.pallas_call(
        finish_kernel,
        out_shape=[jax.ShapeDtypeStruct(a.shape, a.dtype) for a in arrays],
        in_specs=[VMEM] * len(arrays),
        out_specs=[ANY] * len(arrays),
        scratch_shapes=[pltpu.SemaphoreType.DMA((len(arrays),))],
        compiler_params=pltpu.CompilerParams(vmem_limit_bytes=16 << 20),
        name="finish",
    )(*arrays)


def shards(
    features,
    self_weight,
    neigh_weight,
    block_row,
    block_col,
    block_count,
    edge_weight,
    train_mask,
    out_cotangent,
):
    rows = block_row.reshape(512)
    cols = block_col.reshape(512)
    count = block_count.reshape(1)
    mask = train_mask.reshape(4, 128)
    gathered, zf, deg = gather_rows(
        count, block_row.reshape(1, 512), features, edge_weight.reshape(512, 4096)
    )
    raw_part = forward(count, cols, rows, zf, gathered)
    hidden, group, own_term, grads, zt = node(
        raw_part, deg, features, self_weight, neigh_weight, mask, out_cotangent, zf
    )
    through, hidden = backward(count, rows, cols, zt, group, hidden)
    return hidden, *finish(*scatter_rows(through, own_term, grads))


def solution(mesh):
    in_specs = (
        P(("row", "col"), None),
        P(),
        P(),
        P("row", "col", None),
        P("row", "col", None),
        P("row", "col"),
        P("row", "col", None, None),
        P(("row", "col")),
        P(("row", "col"), None),
    )
    out_specs = (P(("row", "col"), None), P(("row", "col"), None), P(), P())
    return jax.shard_map(shards, mesh=mesh, in_specs=in_specs, out_specs=out_specs, check_vma=False)
```

```python
import functools

import jax
import jax.numpy as jnp
from jax import lax
from jax.experimental import pallas as pl
from jax.experimental.pallas import tpu as pltpu
from jax.sharding import PartitionSpec as P

MESH = pl.DeviceIdType.MESH
BF = jnp.bfloat16
F32 = jnp.float32
VMEM = pl.BlockSpec(memory_space=pltpu.VMEM)
SMEM = pl.BlockSpec(memory_space=pltpu.SMEM)
ANY = pl.BlockSpec(memory_space=pl.ANY)
ND = 512
UNROLL = 16
WORK = (8, 3, 3, 2, 2)
TURN = (48, 8)


def place():
    row = lax.axis_index("row")
    return row // 4, (row // 2) % 2, row % 2, lax.axis_index("col")


def greet(targets):
    barrier = pltpu.get_barrier_semaphore()
    for target in targets:
        pl.semaphore_signal(barrier, inc=1, device_id=target, device_id_type=MESH)
    pl.semaphore_wait(barrier, len(targets))


def sender(ss):
    sent = []

    def send(src, dst, sem, target):
        cp = pltpu.make_async_remote_copy(
            src_ref=src,
            dst_ref=dst,
            send_sem=ss.at[len(sent)],
            recv_sem=sem,
            device_id=target,
            device_id_type=MESH,
        )
        cp.start()
        sent.append(cp)
        return cp

    return send, sent


def ring_gather(half, x, table, base, send, zs, ys, along, across, share, idle):
    last = {}

    def go(src, row, lo, n, sem, target):
        return send(
            x.at[pl.ds(lo, n)] if src is x else table.at[pl.ds(row + lo, n)],
            table.at[pl.ds(row + lo, n)],
            sem,
            target,
        )

    own, partner = base(0, 0), base(0, 1)
    first = go(x, own, 0, 256, ys.at[0], across)
    for part in (1, 0):
        for d in range(2):
            last[d, 1, part] = go(x, own, part * 256, 256, zs.at[d, 0, part], along[d])
    crossing = [(go(x, own, 256, 256, ys.at[1], across), partner)]
    share(x, own, 0, 512)
    idle(0)
    first.wait_recv()
    for d in range(2):
        last[d, 1, 2] = go(table, partner, 0, 256, zs.at[d, 0, 2], along[d])
    for step in range(1, half + 1):
        arriving, crossing = crossing, []
        for part in (1, 2, 0):
            for d in range(2):
                if (d, step, part) not in last:
                    continue
                e = 2 * half - step if d == 0 else step
                row = base(e, 0 if part < 2 else 1)
                lo, n = (0, 256, 0)[part], 256
                if step == half and part == 2:
                    lo, n = d * 128, 128
                last[d, step, part].wait_recv()
                if step < half - 1 or (step == half - 1 and part == d):
                    last[d, step + 1, part] = go(table, row, lo, n, zs.at[d, step, part], along[d])
                elif step == half - 1 and part == 2:
                    last[d, half, 2] = go(table, row, d * 128, 128, zs.at[d, step, 2], along[d])
                if part == 1:
                    cp = go(table, row, 256, 256, ys.at[2 * step + d], across)
                    crossing.append((cp, base(e, 1)))
                if step == half:
                    share(table, row, lo, n)
                elif part == 0:
                    share(table, row, 0, 512)
                idle(step)
        for cp, row in arriving:
            cp.wait_recv()
            share(table, row, 0, 512)
    for cp, row in crossing:
        cp.wait_recv()
        share(table, row, 256, 256)


def star_gather(x, table, base, send, xs, ys, along, across, idle):
    def go(src, row, lo, sem, target):
        return send(
            x.at[pl.ds(lo, 256)] if src is x else table.at[pl.ds(row + lo, 256)],
            table.at[pl.ds(row + lo, 256)],
            sem,
            target,
        )

    own, partner = base(0, 0), base(0, 1)
    idle("B")
    second = [go(x, own, 256, xs.at[e - 1, 1], along[e]) for e in (1, 3, 2)]
    rest = [go(x, own, 256, ys.at[0], across)]
    idle("A")
    first = go(x, own, 0, ys.at[4], across)
    rest += [go(x, own, 0, xs.at[e - 1, 0], along[e]) for e in (1, 3, 2)]
    idle("sent")
    first.wait_recv()
    rest += [go(table, partner, 0, xs.at[e - 1, 2], along[e]) for e in (1, 3, 2)]
    idle("partner")
    for cp, e in zip(second, (1, 3, 2)):
        cp.wait_recv()
        rest.append(go(table, base(4 - e, 0), 256, ys.at[e], across))
    idle("last")
    for cp in rest:
        cp.wait_recv()


def ring_reduce(half, value, direct, zsrc, rz, send, zs, along):
    zsent = {}

    def arrived(d, step, part, lo, n):
        return rz[d, step, part * 256 + lo : part * 256 + lo + n, :].astype(F32)

    def piece(d, step, part):
        e = (2 * half - step) if d == 0 else step
        lo, n = (0, 256) if (step < half or part < 2) else (d * 128, 128)
        at = pl.ds(part * 256 + lo, n)
        alone = step == half or (step == half - 1 and part == 1 - d)
        src = direct(e, part, lo, n) if alone else None
        if src is None:
            total = value(e, part, lo, n)
            if step < half - 1 or (step == half - 1 and part == d):
                zsent[d, step + 1, part].wait_recv()
                total = total + arrived(d, step, part, 0, 256)
            elif step == half - 1 and part == 2:
                zsent[d, half, 2].wait_recv()
                halves = [total[:128], total[128:]]
                halves[d] = halves[d] + arrived(d, step, 2, d * 128, 128)
                total = jnp.concatenate(halves, 0)
            zsrc[d, step - 1, at, :] = total.astype(BF)
            src = zsrc.at[d, step - 1, at]
        zsent[d, step, part] = send(src, rz.at[d, step - 1, at], zs.at[d, step - 1, part], along[d])

    def final(part):
        total = value(0, part, 0, 256)
        for d in range(2):
            zsent[d, 1, part].wait_recv()
            total = total + arrived(d, 0, part, 0, 256)
        return total

    return piece, final


def gather_kernel(
    cnt, rows_hbm, x, w,
    g, zf, deg,
    wv, rows, pat, dsl, ss, zs, ys, ks, ls, wsem,
):
    z, yl, k, col = place()

    def dev(zz, yy, kk):
        return (zz * 4 + yy * 2 + kk, col)

    slabs = []
    for i in range(8):
        slabs.append(pltpu.make_async_copy(w.at[pl.ds(i * 64, 64)], wv.at[pl.ds(i * 64, 64)], wsem.at[i]))
        slabs[-1].start()
    names = pltpu.make_async_copy(rows_hbm, rows, ls.at[1])
    names.start()
    along = (dev(lax.rem(z + 1, 8), yl, k), dev(lax.rem(z + 7, 8), yl, k))
    across, sibling = dev(z, 1 - yl, k), dev(z, yl, 1 - k)
    greet((*along, across, sibling))
    send, sent = sender(ss)

    def base(e, r):
        yy = yl if r == 0 else 1 - yl
        return pl.multiple_of((lax.rem(z + e, 8) * 4 + yy * 2 + k) * ND, ND)

    to_sibling = []

    def share(src, row, lo, n):
        at = pl.ds(row + lo, n)
        src = x.at[pl.ds(lo, n)] if src is x else g.at[at]
        to_sibling.append(send(src, g.at[at], ks.at[len(to_sibling)], sibling))

    low = lax.broadcasted_iota(jnp.int32, (32, 128), 1) < 64
    lim = cnt[0]
    done = [0]

    def unit(i):
        b = pl.multiple_of(i * 8, 8)
        live = (b + lax.broadcasted_iota(jnp.int32, (8, 4096), 0)) < lim
        y = jnp.where(live, wv[pl.ds(b, 8), :], 0).astype(F32).reshape(8, 32, 128)
        for h4 in range(2):
            y4 = [y[h4 * 4 + s] for s in range(4)]
            r4 = [pltpu.roll(v, 64, 1) for v in y4]
            zf[i * 2 + h4] = jnp.concatenate(
                [
                    jnp.where(low, y4[0], r4[2]),
                    jnp.where(low, r4[0], y4[2]),
                    jnp.where(low, y4[1], r4[3]),
                    jnp.where(low, r4[1], y4[3]),
                ],
                0,
            ).astype(BF)

    def work(n):
        n = min(n, 64 - done[0])
        if n <= 0:
            return
        lo = done[0]
        for i in range(lo // 8 if lo % 8 == 0 else lo // 8 + 1, (lo + n - 1) // 8 + 1):
            slabs[i].wait()
        pl.loop(lo, lo + n)(unit)
        for i in range(lo // 8, (lo + n) // 8):
            at = pl.ds(i * 64, 64)
            dsl[at, :] = jnp.dot(
                wv[at, :].astype(F32).astype(BF), pat[...], preferred_element_type=F32
            ).astype(BF)
        done[0] += n

    def idle(step):
        work(WORK[step])

    def prepare(step):
        if step == 0:
            at = lax.broadcasted_iota(jnp.int32, (4096, 128), 0) // 64
            pat[...] = (at == lax.broadcasted_iota(jnp.int32, (4096, 128), 1)).astype(BF)
        idle(step)

    mine = pltpu.make_async_copy(x, g.at[pl.ds(base(0, 0), ND)], ls.at[0])
    mine.start()
    ring_gather(4, x, g, base, send, zs, ys, along, across, share, prepare)
    work(64)
    names.wait()
    slot = lax.broadcasted_iota(jnp.int32, (64, 512), 1)
    hot = (lax.broadcasted_iota(jnp.int32, (64, 512), 0) == rows[...]) & (slot < lim)
    deg[...] = jnp.dot(hot.astype(F32).astype(BF), dsl[...], preferred_element_type=F32)
    for cp in to_sibling:
        cp.wait_recv()
    for cp in sent:
        cp.wait_send()
    mine.wait()


def gather_rows(count, rows, x, w):
    rows = pltpu.with_memory_space_constraint(rows, pltpu.HBM)
    x = pltpu.with_memory_space_constraint(x, pltpu.HBM)
    w = pltpu.with_memory_space_constraint(w, pltpu.HBM)
    return pl.pallas_call(
        gather_kernel,
        out_shape=[
            jax.ShapeDtypeStruct((32 * ND, 128), BF),
            jax.ShapeDtypeStruct((128, 128, 128), BF),
            jax.ShapeDtypeStruct((64, 128), F32),
        ],
        in_specs=[SMEM, ANY, ANY, ANY],
        out_specs=[ANY, VMEM, VMEM],
        scratch_shapes=[
            pltpu.VMEM((512, 4096), jnp.int32),
            pltpu.VMEM((1, 512), jnp.int32),
            pltpu.VMEM((4096, 128), BF),
            pltpu.VMEM((512, 128), BF),
            pltpu.SemaphoreType.DMA((80,)),
            pltpu.SemaphoreType.DMA((2, 4, 3)),
            pltpu.SemaphoreType.DMA((10,)),
            pltpu.SemaphoreType.DMA((40,)),
            pltpu.SemaphoreType.DMA((2,)),
            pltpu.SemaphoreType.DMA((8,)),
        ],
        compiler_params=pltpu.CompilerParams(
            collective_id=0, has_side_effects=True, vmem_limit_bytes=43 << 20
        ),
        name="gather_rows",
    )(count, rows, x, w)


def two_blocks(a, b):
    zero = jnp.zeros((64, 128), BF)
    return jnp.concatenate(
        [jnp.concatenate([a, zero], 1), jnp.concatenate([zero, b], 1)], 0
    )


def spread_kernel(near, far, cnt, frm, to, blocks, table, out, acc):
    acc[...] = jnp.zeros_like(acc)

    def block(ref, s):
        return pl.ds(pl.multiple_of(ref[s] * 64, 64), 64)

    @pl.loop(0, (cnt[0] + 4 * UNROLL - 1) // (4 * UNROLL))
    def _(i):
        parts = []
        for u in range(UNROLL):
            g = i * UNROLL + u
            for half in range(2):
                first = 4 * g + near * half
                second = first + far
                both = two_blocks(table[block(frm, first), :], table[block(frm, second), :])
                lhs = blocks[g, half * 64 : half * 64 + 64, :]
                prod = jnp.dot(lhs, both, preferred_element_type=F32)
                parts.append((first, prod[:, :128]))
                parts.append((second, prod[:, 128:]))
        for s, value in parts:
            acc[block(to, s), :] += value

    out[...] = acc[...].astype(BF)


def forward(count, frm, to, blocks, table):
    return pl.pallas_call(
        functools.partial(spread_kernel, 1, 2),
        out_shape=jax.ShapeDtypeStruct((8 * ND, 128), BF),
        in_specs=[SMEM, SMEM, SMEM, VMEM, VMEM],
        out_specs=VMEM,
        scratch_shapes=[pltpu.VMEM((8 * ND, 128), F32)],
        compiler_params=pltpu.CompilerParams(vmem_limit_bytes=16 << 20),
        name="forward",
    )(count, frm, to, blocks, table)


def backward_kernel(cnt, frm, to, blocks, table, hidden, out, kept, acc, sem):
    keep = pltpu.make_async_copy(hidden, kept, sem)
    keep.start()
    spread_kernel(2, 1, cnt, frm, to, blocks, table, out, acc)
    keep.wait()


def backward(count, frm, to, blocks, table, hidden):
    return pl.pallas_call(
        backward_kernel,
        out_shape=[
            jax.ShapeDtypeStruct((32 * ND, 128), BF),
            jax.ShapeDtypeStruct(hidden.shape, hidden.dtype),
        ],
        in_specs=[SMEM, SMEM, SMEM, VMEM, VMEM, ANY],
        out_specs=[VMEM, ANY],
        scratch_shapes=[pltpu.VMEM((32 * ND, 128), F32), pltpu.SemaphoreType.DMA],
        compiler_params=pltpu.CompilerParams(vmem_limit_bytes=20 << 20),
        name="backward",
    )(count, frm, to, blocks, table, hidden)


def upright(rows, width):
    eye = lax.broadcasted_iota(jnp.int32, (width, 128), 0) == lax.broadcasted_iota(
        jnp.int32, (width, 128), 1
    )
    return jnp.concatenate(
        [
            jnp.sum(jnp.where(eye, rows[i : i + 1, :], 0.0), axis=1, keepdims=True)
            for i in range(rows.shape[0])
        ],
        0,
    )


def node_kernel(
    raw_part, deg, x, ws, wn, mask, cot, zf,
    hidden, group, own_term, gsum, zt,
    yb, xsrc, rx, fsrc, fy, rd, nat, sc, grads, gr, ss, x1, y1, x2, y2, ds, gsem, ls,
):
    row, col = lax.axis_index("row"), lax.axis_index("col")
    yh, xx = col // 4, lax.rem(col, 4)
    z, side = row // 4, lax.rem(row, 4)
    zat = [lax.rem(z + e, 8) for e in range(8)]
    xat = [lax.rem(xx + e, 4) for e in range(4)]
    peers = [lax.rem(col + o, 8) for o in range(8)]
    along = [(row, yh * 4 + xat[e]) for e in range(4)]
    across = (row, (1 - yh) * 4 + xx)
    greet([(row, p) for p in peers[1:]] + [(zat[e] * 4 + side, col) for e in range(1, 8)])
    send, sent = sender(ss)

    def base(e, r):
        return pl.multiple_of(((yh if r == 0 else 1 - yh) * 4 + xat[e]) * ND, ND)

    def mine(e, r, lo):
        return raw_part.at[pl.ds(base(e, r) + lo, 256)]

    ysent = {e: send(mine(e, 1, 256), yb.at[e], y1.at[e], across) for e in (2, 1, 3)}
    xsent = {}
    for part in (2, 0):
        for e in (2, 1, 3):
            src = mine(e, 1 if part == 2 else 0, 0)
            xsent[e, part] = send(src, rx.at[e - 1, part], x1.at[e - 1, part], along[e])
            if part == 2 and e == 2:
                ysent[0] = send(mine(0, 1, 256), yb.at[0], y1.at[0], across)
    degs = []
    for o in range(1, 8):
        src = deg.at[pl.ds(pl.multiple_of(peers[o] * 8, 8), 8)]
        degs.append(send(src, rd.at[o], ds.at[o], (row, peers[o])))

    def pass_on(e):
        ysent[e].wait_recv()
        xsrc[e - 1] = (mine(e, 0, 256)[...].astype(F32) + yb[e].astype(F32)).astype(BF)
        xsent[e, 1] = send(xsrc.at[e - 1], rx.at[e - 1, 1], x1.at[e - 1, 1], along[e])

    def final(part, total):
        for e in (2, 1, 3):
            xsent[e, part].wait_recv()
            total = total + rx[e - 1, part].astype(F32)
        return total

    pass_on(2)
    pass_on(1)
    pass_on(3)
    fsrc[...] = final(2, mine(0, 1, 0)[...].astype(F32)).astype(BF)
    last = send(fsrc, fy, y1.at[4], across)
    rd[0] = deg[pl.ds(pl.multiple_of(col * 8, 8), 8), :]
    keep = upright(mask[...].astype(F32), 128)
    for cp in degs:
        cp.wait_recv()
    inverse = 1.0 / upright(jnp.sum(rd[...], axis=0), 64)
    nt = (((1,), (1,)), ((), ()))
    tn = (((0,), (0,)), ((), ()))
    halves = {}

    def layer(lo, raw):
        at = pl.ds(lo, 256)
        raw = raw.reshape(4, 2, 32, 128)
        for p in range(2):
            nat[pl.ds(lo + p, 128, stride=2), :] = raw[:, p].reshape(128, 128)
        inv = inverse[lo : lo + 256]
        agg = (nat[at, :] * inv).astype(BF)
        feats = x[at, :]
        pre = jnp.dot(feats, ws[...], preferred_element_type=F32)
        pre = pre + jnp.dot(agg, wn[...], preferred_element_type=F32)
        sig = jax.nn.sigmoid(pre)
        slope = sig * (1.0 + pre * (1.0 - sig))
        dpre = (cot[at, :].astype(F32) * keep[lo : lo + 256] * slope).astype(BF)
        nat[at, :] = lax.dot_general(dpre, wn[...], nt, preferred_element_type=F32) * inv
        for p in range(2):
            part = nat[pl.ds(lo + p, 128, stride=2), :].astype(BF).reshape(4, 32, 128)
            for i in range(4):
                sc[lo + i * 64 + p * 32 : lo + i * 64 + p * 32 + 32, :] = part[i]
        hidden[at, :] = (pre * sig).astype(BF)
        halves[lo] = feats, agg, dpre

    slices = []

    def later():
        g_self, g_neigh = 0.0, 0.0
        for lo, (feats, agg, dpre) in halves.items():
            own_term[lo : lo + 256, :] = lax.dot_general(dpre, ws[...], nt, preferred_element_type=F32)
            g_self = g_self + lax.dot_general(feats, dpre, tn, preferred_element_type=F32)
            g_neigh = g_neigh + lax.dot_general(agg, dpre, tn, preferred_element_type=F32)
        for i, v in enumerate((g_self[:, :128], g_self[:, 128:], g_neigh[:, :128], g_neigh[:, 128:])):
            grads[i * 128 : i * 128 + 128, :] = v
        for e in range(1, 8):
            src = grads.at[pl.ds(pl.multiple_of(zat[e] * 64, 64), 64)]
            slices.append(send(src, gr.at[e], gsem.at[e], (zat[e] * 4 + side, col)))

    turned = [0]

    def turn(n):
        lo = turned[0]
        turned[0] += n

        @pl.loop(lo, lo + n)
        def _(i):
            zt[i] = zf[i].T

    stay = pltpu.make_async_copy(sc, group.at[pl.ds(base(0, 0), ND)], ls)

    def idle(when):
        if when == "B":
            ysent[0].wait_recv()
            layer(256, final(1, mine(0, 0, 256)[...].astype(F32) + yb[0].astype(F32)))
        elif when == "A":
            first = final(0, mine(0, 0, 0)[...].astype(F32))
            last.wait_recv()
            layer(0, first + fy[...].astype(F32))
        elif when == "sent":
            stay.start()
            turn(TURN[0])
        elif when == "partner":
            turn(TURN[1])
        else:
            later()
            turn(128 - TURN[0] - TURN[1])

    star_gather(sc, group, base, send, x2, y2, along, across, idle)
    total = grads[pl.ds(pl.multiple_of(z * 64, 64), 64), :]
    for e in range(1, 8):
        slices[e - 1].wait_recv()
        total = total + gr[e]
    gsum[...] = total
    stay.wait()
    for cp in sent:
        cp.wait_send()


def node(raw_part, deg, x, ws, wn, mask, cot, zf):
    return pl.pallas_call(
        node_kernel,
        out_shape=[
            jax.ShapeDtypeStruct((ND, 256), BF),
            jax.ShapeDtypeStruct((8 * ND, 128), BF),
            jax.ShapeDtypeStruct((ND, 128), F32),
            jax.ShapeDtypeStruct((64, 128), F32),
            jax.ShapeDtypeStruct((128, 128, 128), BF),
        ],
        in_specs=[VMEM] * 8,
        out_specs=[VMEM, ANY, VMEM, VMEM, VMEM],
        scratch_shapes=[
            pltpu.VMEM((4, 256, 128), BF),
            pltpu.VMEM((3, 256, 128), BF),
            pltpu.VMEM((3, 3, 256, 128), BF),
            pltpu.VMEM((256, 128), BF),
            pltpu.VMEM((256, 128), BF),
            pltpu.VMEM((8, 8, 128), F32),
            pltpu.VMEM((ND, 128), F32),
            pltpu.VMEM((ND, 128), BF),
            pltpu.VMEM((512, 128), F32),
            pltpu.VMEM((8, 64, 128), F32),
            pltpu.SemaphoreType.DMA((60,)),
            pltpu.SemaphoreType.DMA((3, 3)),
            pltpu.SemaphoreType.DMA((5,)),
            pltpu.SemaphoreType.DMA((3, 3)),
            pltpu.SemaphoreType.DMA((5,)),
            pltpu.SemaphoreType.DMA((8,)),
            pltpu.SemaphoreType.DMA((8,)),
            pltpu.SemaphoreType.DMA,
        ],
        compiler_params=pltpu.CompilerParams(
            collective_id=1, has_side_effects=True, vmem_limit_bytes=20 << 20
        ),
        name="node",
    )(raw_part, deg, x, ws, wn, mask, cot, zf)


def in_order(parts, me, n):
    total = None
    for p in range(n):
        i = lax.rem(me - p - 1 + 2 * n, n)
        total = parts[i] if total is None else total + parts[i]
    return total


def scatter_kernel(
    t, own_term, gpart,
    out, grad_self, grad_neigh,
    sib, ysrc, yb, zsrc, rz, fsrc, fy, gk, gx, gy, gsrc, gall,
    ss, zs, ys, ks, q0, q1, q2, q3,
):
    z, yl, k, col = place()

    def dev(zz, yy, kk, cc=None):
        return (zz * 4 + yy * 2 + kk, col if cc is None else cc)

    zat = [lax.rem(z + e, 8) for e in range(8)]
    yh, xx = col // 4, lax.rem(col, 4)
    along = (dev(zat[7], yl, k), dev(zat[1], yl, k))
    across, sibling = dev(z, 1 - yl, k), dev(z, yl, 1 - k)
    far = (1 - yh) * 4 + xx
    ypeers = (across, dev(z, yl, k, far), dev(z, 1 - yl, k, far))
    xpeers = [dev(z, yl, k, yh * 4 + lax.rem(xx + e, 4)) for e in (1, 2, 3)]
    zpeers = [dev(zat[e], yl, k) for e in range(1, 8)]
    greet([sibling, *ypeers, *xpeers, *zpeers])
    send, sent = sender(ss)
    theirs = pl.ds(pl.multiple_of((1 - k) * 32, 32), 32)
    ours = pl.ds(pl.multiple_of(k * 32, 32), 32)
    halves = send(gpart.at[theirs], gk, q0.at[0], sibling)

    sibs = {}
    for e in (4, 3, 5, 2, 6, 1, 7, 0):
        sibs[e] = send(t.at[zat[e], :, 1 - k], sib.at[e], ks.at[e], sibling)
    ready = set()

    def mine(e, r, lo, n):
        if e not in ready:
            sibs[e].wait_recv()
            ready.add(e)
        yy = yl if r == 0 else 1 - yl
        at = pl.ds(lo, n)
        return t[zat[e], yy, k, at, :].astype(F32) + sib[e, yy, at, :].astype(F32)

    ysent = {}

    def cross(e):
        ysrc[e] = mine(e, 1, 256, 256).astype(BF)
        ysent[e] = send(ysrc.at[e], yb.at[e], ys.at[e], across)

    crossed = set()

    def value(e, part, lo, n):
        if part == 2:
            return mine(e, 1, lo, n)
        if part == 0:
            return mine(e, 0, lo, n)
        if e not in crossed:
            ysent[e].wait_recv()
            crossed.add(e)
        return mine(e, 0, 256 + lo, n) + yb[e, lo : lo + n, :].astype(F32)

    piece, final = ring_reduce(4, value, lambda *a: None, zsrc, rz, send, zs, along)

    cross(4)
    piece(0, 4, 2)
    piece(1, 4, 2)
    piece(0, 4, 0)
    cross(3)
    cross(5)
    piece(1, 4, 1)
    cross(2)
    cross(6)
    cross(1)
    cross(7)
    cross(0)
    halves.wait_recv()
    total = gpart[pl.ds(pl.multiple_of(k * 32, 32), 32), :] + gk[...]
    gsrc[0] = total
    swaps = [send(gsrc.at[0], gx.at[i], q1.at[i], xpeers[i]) for i in range(3)]
    for part in (2, 0, 1):
        for d in range(2):
            piece(d, 3, part)
    gx[3] = gsrc[0]
    for cp in swaps:
        cp.wait_recv()
    total = in_order(gx, xx, 4)
    gsrc[1] = total
    swaps = [send(gsrc.at[1], gy.at[i], q2.at[i], ypeers[i]) for i in range(3)]
    for part in (2, 0, 1):
        for d in range(2):
            piece(d, 2, part)
    for cp in swaps:
        cp.wait_recv()
    total = (gsrc[1] + gy[0]) + (gy[1] + gy[2])
    mine_at = gall.at[z, k]
    gall[z, k] = total
    swaps = [send(mine_at, mine_at, q3.at[i], zpeers[i]) for i in range(7)]
    for part in (2, 0, 1):
        for d in range(2):
            piece(d, 1, part)
    fsrc[...] = final(2).astype(BF)
    last = send(fsrc, fy, ys.at[8], across)
    first = final(0) + own_term[:256, :]
    out[256:, :] = (final(1) + own_term[256:, :]).astype(BF)
    for cp in swaps:
        cp.wait_recv()
    other = send(gall.at[:, k], gall.at[:, k], q0.at[1], sibling)
    last.wait_recv()
    out[:256, :] = (first + fy[...].astype(F32)).astype(BF)
    other.wait_recv()
    for i, ref in enumerate((grad_self, grad_neigh)):
        for h in range(2):
            lo = i * 4 + h * 2
            ref[:, h * 128 : h * 128 + 128] = gall[lo : lo + 2].reshape(128, 128)
    for cp in sent:
        cp.wait_send()


def scatter_rows(t, own_term, grads):
    return pl.pallas_call(
        scatter_kernel,
        out_shape=[
            jax.ShapeDtypeStruct((ND, 128), BF),
            jax.ShapeDtypeStruct((128, 256), F32),
            jax.ShapeDtypeStruct((128, 256), F32),
        ],
        in_specs=[VMEM, VMEM, VMEM],
        out_specs=[VMEM, VMEM, VMEM],
        scratch_shapes=[
            pltpu.VMEM((8, 2, ND, 128), BF),
            pltpu.VMEM((8, 256, 128), BF),
            pltpu.VMEM((8, 256, 128), BF),
            pltpu.VMEM((2, 4, 768, 128), BF),
            pltpu.VMEM((2, 4, 768, 128), BF),
            pltpu.VMEM((256, 128), BF),
            pltpu.VMEM((256, 128), BF),
            pltpu.VMEM((32, 128), F32),
            pltpu.VMEM((4, 32, 128), F32),
            pltpu.VMEM((3, 32, 128), F32),
            pltpu.VMEM((2, 32, 128), F32),
            pltpu.VMEM((8, 2, 32, 128), F32),
            pltpu.SemaphoreType.DMA((90,)),
            pltpu.SemaphoreType.DMA((2, 4, 3)),
            pltpu.SemaphoreType.DMA((9,)),
            pltpu.SemaphoreType.DMA((8,)),
            pltpu.SemaphoreType.DMA((2,)),
            pltpu.SemaphoreType.DMA((3,)),
            pltpu.SemaphoreType.DMA((3,)),
            pltpu.SemaphoreType.DMA((7,)),
        ],
        compiler_params=pltpu.CompilerParams(
            collective_id=2, has_side_effects=True, vmem_limit_bytes=20 << 20
        ),
        name="scatter_rows",
    )(t.reshape(8, 2, 2, ND, 128), own_term, grads)


def finish_kernel(*refs):
    n = len(refs) // 2
    sem = refs[-1]
    copies = [pltpu.make_async_copy(refs[i], refs[n + i], sem.at[i]) for i in range(n)]
    for cp in copies:
        cp.start()
    for cp in copies:
        cp.wait()


def finish(*arrays):
    return pl.pallas_call(
        finish_kernel,
        out_shape=[jax.ShapeDtypeStruct(a.shape, a.dtype) for a in arrays],
        in_specs=[VMEM] * len(arrays),
        out_specs=[ANY] * len(arrays),
        scratch_shapes=[pltpu.SemaphoreType.DMA((len(arrays),))],
        compiler_params=pltpu.CompilerParams(vmem_limit_bytes=16 << 20),
        name="finish",
    )(*arrays)


def shards(
    features,
    self_weight,
    neigh_weight,
    block_row,
    block_col,
    block_count,
    edge_weight,
    train_mask,
    out_cotangent,
):
    rows = block_row.reshape(512)
    cols = block_col.reshape(512)
    count = block_count.reshape(1)
    mask = train_mask.reshape(4, 128)
    gathered, zf, deg = gather_rows(
        count, block_row.reshape(1, 512), features, edge_weight.reshape(512, 4096)
    )
    raw_part = forward(count, cols, rows, zf, gathered)
    hidden, group, own_term, grads, zt = node(
        raw_part, deg, features, self_weight, neigh_weight, mask, out_cotangent, zf
    )
    through, hidden = backward(count, rows, cols, zt, group, hidden)
    return hidden, *finish(*scatter_rows(through, own_term, grads))


def solution(mesh):
    in_specs = (
        P(("row", "col"), None),
        P(),
        P(),
        P("row", "col", None),
        P("row", "col", None),
        P("row", "col"),
        P("row", "col", None, None),
        P(("row", "col")),
        P(("row", "col"), None),
    )
    out_specs = (P(("row", "col"), None), P(("row", "col"), None), P(), P())
    return jax.shard_map(shards, mesh=mesh, in_specs=in_specs, out_specs=out_specs, check_vma=False)
```

```python
import functools

import jax
import jax.numpy as jnp
from jax import lax
from jax.experimental import pallas as pl
from jax.experimental.pallas import tpu as pltpu
from jax.sharding import PartitionSpec as P

MESH = pl.DeviceIdType.MESH
BF = jnp.bfloat16
F32 = jnp.float32
VMEM = pl.BlockSpec(memory_space=pltpu.VMEM)
SMEM = pl.BlockSpec(memory_space=pltpu.SMEM)
ANY = pl.BlockSpec(memory_space=pl.ANY)
ND = 512
UNROLL = 32
WORK = (8, 3, 3, 3, 1)
TURN = (32,)


def place():
    row = lax.axis_index("row")
    return row // 4, (row // 2) % 2, row % 2, lax.axis_index("col")


def greet(targets, meanwhile=None):
    barrier = pltpu.get_barrier_semaphore()
    for target in targets:
        pl.semaphore_signal(barrier, inc=1, device_id=target, device_id_type=MESH)
    if meanwhile is not None:
        meanwhile()
    pl.semaphore_wait(barrier, len(targets))


def sender(ss):
    sent = []

    def send(src, dst, sem, target):
        cp = pltpu.make_async_remote_copy(
            src_ref=src,
            dst_ref=dst,
            send_sem=ss.at[len(sent)],
            recv_sem=sem,
            device_id=target,
            device_id_type=MESH,
        )
        cp.start()
        sent.append(cp)
        return cp

    return send, sent


def ring_gather(half, x, table, base, send, zs, ys, along, across, share, idle):
    last = {}

    def go(src, row, lo, n, sem, target):
        return send(
            x.at[pl.ds(lo, n)] if src is x else table.at[pl.ds(row + lo, n)],
            table.at[pl.ds(row + lo, n)],
            sem,
            target,
        )

    own, partner = base(0, 0), base(0, 1)
    first = [go(x, own, 128 * i, 128, ys.at[0, i], across) for i in range(2)]
    for part in (1, 0):
        for i in range(2):
            for d in range(2):
                lo = part * 256 + i * 128
                last[d, 1, part, i] = go(x, own, lo, 128, zs.at[d, 0, part, i], along[d])
    crossing = [([go(x, own, 256, 256, ys.at[1, 0], across)], partner)]
    share(x, own, 0, 512)
    idle(0)
    for i in range(2):
        first[i].wait_recv()
        for d in range(2):
            last[d, 1, 2, i] = go(table, partner, 128 * i, 128, zs.at[d, 0, 2, i], along[d])
    for step in range(1, half + 1):
        arriving, crossing = crossing, []
        crossed = ([], [])
        for part, i in ((1, 0), (1, 1), (2, 0), (2, 1), (0, 0), (0, 1)):
            for d in range(2):
                if (d, step, part, i) not in last:
                    continue
                e = 2 * half - step if d == 0 else step
                row = base(e, 0 if part < 2 else 1)
                lo = (0, 256, 0)[part] + 128 * i
                last[d, step, part, i].wait_recv()
                goes = step < half - 1
                if step == half - 1:
                    goes = part == d or (part == 2 and i == d)
                if goes:
                    last[d, step + 1, part, i] = go(
                        table, row, lo, 128, zs.at[d, step, part, i], along[d]
                    )
                if part == 1:
                    cp = go(table, row, lo, 128, ys.at[2 * step + d, i], across)
                    crossed[d].append(cp)
                    if i == 1:
                        crossing.append((crossed[d], base(e, 1)))
                if step == half:
                    share(table, row, lo, 128)
                elif part == 0 and i == 1:
                    share(table, row, 0, 512)
            idle(step)
        for cps, row in arriving:
            for cp in cps:
                cp.wait_recv()
            share(table, row, 0, 512)
    for cps, row in crossing:
        for i, cp in enumerate(cps):
            cp.wait_recv()
            share(table, row, 256 + 128 * i, 128)


def star_gather(x, table, base, send, xs, ys, along, across, idle):
    def go(src, row, lo, sem, target):
        return send(
            x.at[pl.ds(lo, 256)] if src is x else table.at[pl.ds(row + lo, 256)],
            table.at[pl.ds(row + lo, 256)],
            sem,
            target,
        )

    own, partner = base(0, 0), base(0, 1)
    idle("B")
    second = [go(x, own, 256, xs.at[e - 1, 1], along[e]) for e in (1, 3, 2)]
    rest = [go(x, own, 256, ys.at[0], across)]
    idle("A")
    first = go(x, own, 0, ys.at[4], across)
    rest += [go(x, own, 0, xs.at[e - 1, 0], along[e]) for e in (1, 3, 2)]
    idle("sent")
    first.wait_recv()
    rest += [go(table, partner, 0, xs.at[e - 1, 2], along[e]) for e in (1, 3, 2)]
    idle("partner")
    for cp, e in zip(second, (1, 3, 2)):
        cp.wait_recv()
        rest.append(go(table, base(4 - e, 0), 256, ys.at[e], across))
    idle("last")
    for cp in rest:
        cp.wait_recv()


def ring_reduce(half, value, direct, zsrc, rz, send, zs, along):
    zsent = {}

    def arrived(d, step, part, lo, n):
        return rz[d, step, part * 256 + lo : part * 256 + lo + n, :].astype(F32)

    def piece(d, step, part):
        e = (2 * half - step) if d == 0 else step
        lo, n = (0, 256) if (step < half or part < 2) else (d * 128, 128)
        at = pl.ds(part * 256 + lo, n)
        alone = step == half or (step == half - 1 and part == 1 - d)
        src = direct(e, part, lo, n) if alone else None
        if src is None:
            total = value(e, part, lo, n)
            if step < half - 1 or (step == half - 1 and part == d):
                zsent[d, step + 1, part].wait_recv()
                total = total + arrived(d, step, part, 0, 256)
            elif step == half - 1 and part == 2:
                zsent[d, half, 2].wait_recv()
                halves = [total[:128], total[128:]]
                halves[d] = halves[d] + arrived(d, step, 2, d * 128, 128)
                total = jnp.concatenate(halves, 0)
            zsrc[d, step - 1, at, :] = total.astype(BF)
            src = zsrc.at[d, step - 1, at]
        zsent[d, step, part] = send(src, rz.at[d, step - 1, at], zs.at[d, step - 1, part], along[d])

    def final(part):
        total = value(0, part, 0, 256)
        for d in range(2):
            zsent[d, 1, part].wait_recv()
            total = total + arrived(d, 0, part, 0, 256)
        return total

    return piece, final


def gather_kernel(
    cnt, rows_hbm, x, w,
    g, zf, deg,
    wv, rows, pat, dsl, ss, zs, ys, ks, ls, wsem,
):
    z, yl, k, col = place()

    def dev(zz, yy, kk):
        return (zz * 4 + yy * 2 + kk, col)

    along = (dev(lax.rem(z + 1, 8), yl, k), dev(lax.rem(z + 7, 8), yl, k))
    across, sibling = dev(z, 1 - yl, k), dev(z, yl, 1 - k)
    slabs = [
        pltpu.make_async_copy(w.at[pl.ds(i * 64, 64)], wv.at[pl.ds(i * 64, 64)], wsem.at[i])
        for i in range(8)
    ]
    names = pltpu.make_async_copy(rows_hbm, rows, ls.at[1])

    def fetch():
        for cp in (*slabs, names):
            cp.start()
        at = lax.broadcasted_iota(jnp.int32, (4096, 128), 0) // 64
        pat[...] = (at == lax.broadcasted_iota(jnp.int32, (4096, 128), 1)).astype(BF)

    greet((*along, across, sibling), fetch)
    send, sent = sender(ss)

    def base(e, r):
        yy = yl if r == 0 else 1 - yl
        return pl.multiple_of((lax.rem(z + e, 8) * 4 + yy * 2 + k) * ND, ND)

    to_sibling = []

    def share(src, row, lo, n):
        at = pl.ds(row + lo, n)
        src = x.at[pl.ds(lo, n)] if src is x else g.at[at]
        to_sibling.append(send(src, g.at[at], ks.at[len(to_sibling)], sibling))

    low = lax.broadcasted_iota(jnp.int32, (32, 128), 1) < 64
    lim = cnt[0]
    done = [0]

    def unit(i):
        b = pl.multiple_of(i * 8, 8)
        live = (b + lax.broadcasted_iota(jnp.int32, (8, 4096), 0)) < lim
        y = jnp.where(live, wv[pl.ds(b, 8), :], 0).astype(F32).reshape(8, 32, 128)
        for h4 in range(2):
            y4 = [y[h4 * 4 + s] for s in range(4)]
            r4 = [pltpu.roll(v, 64, 1) for v in y4]
            zf[i * 2 + h4] = jnp.concatenate(
                [
                    jnp.where(low, y4[0], r4[2]),
                    jnp.where(low, r4[0], y4[2]),
                    jnp.where(low, y4[1], r4[3]),
                    jnp.where(low, r4[1], y4[3]),
                ],
                0,
            ).astype(BF)

    def work(n):
        n = min(n, 64 - done[0])
        if n <= 0:
            return
        lo = done[0]
        for i in range(lo // 8 if lo % 8 == 0 else lo // 8 + 1, (lo + n - 1) // 8 + 1):
            slabs[i].wait()
        pl.loop(lo, lo + n)(unit)
        for i in range(lo // 8, (lo + n) // 8):
            at = pl.ds(i * 64, 64)
            dsl[at, :] = jnp.dot(
                wv[at, :].astype(F32).astype(BF), pat[...], preferred_element_type=F32
            ).astype(BF)
        done[0] += n

    def idle(step):
        work(WORK[step])

    mine = pltpu.make_async_copy(x, g.at[pl.ds(base(0, 0), ND)], ls.at[0])
    mine.start()
    ring_gather(4, x, g, base, send, zs, ys, along, across, share, idle)
    work(64)
    names.wait()
    slot = lax.broadcasted_iota(jnp.int32, (64, 512), 1)
    hot = (lax.broadcasted_iota(jnp.int32, (64, 512), 0) == rows[...]) & (slot < lim)
    deg[...] = jnp.dot(hot.astype(F32).astype(BF), dsl[...], preferred_element_type=F32)
    for cp in to_sibling:
        cp.wait_recv()
    for cp in sent:
        cp.wait_send()
    mine.wait()


def gather_rows(count, rows, x, w):
    rows = pltpu.with_memory_space_constraint(rows, pltpu.HBM)
    x = pltpu.with_memory_space_constraint(x, pltpu.HBM)
    w = pltpu.with_memory_space_constraint(w, pltpu.HBM)
    return pl.pallas_call(
        gather_kernel,
        out_shape=[
            jax.ShapeDtypeStruct((32 * ND, 128), BF),
            jax.ShapeDtypeStruct((128, 128, 128), BF),
            jax.ShapeDtypeStruct((64, 128), F32),
        ],
        in_specs=[SMEM, ANY, ANY, ANY],
        out_specs=[ANY, VMEM, VMEM],
        scratch_shapes=[
            pltpu.VMEM((512, 4096), jnp.int32),
            pltpu.VMEM((1, 512), jnp.int32),
            pltpu.VMEM((4096, 128), BF),
            pltpu.VMEM((512, 128), BF),
            pltpu.SemaphoreType.DMA((110,)),
            pltpu.SemaphoreType.DMA((2, 4, 3, 2)),
            pltpu.SemaphoreType.DMA((10, 2)),
            pltpu.SemaphoreType.DMA((40,)),
            pltpu.SemaphoreType.DMA((2,)),
            pltpu.SemaphoreType.DMA((8,)),
        ],
        compiler_params=pltpu.CompilerParams(
            collective_id=0, has_side_effects=True, vmem_limit_bytes=43 << 20
        ),
        name="gather_rows",
    )(count, rows, x, w)


def two_blocks(a, b):
    zero = jnp.zeros((64, 128), BF)
    return jnp.concatenate(
        [jnp.concatenate([a, zero], 1), jnp.concatenate([zero, b], 1)], 0
    )


def spread_kernel(near, far, cnt, frm, to, blocks, table, out, acc):
    acc[...] = jnp.zeros_like(acc)

    def block(ref, s):
        return pl.ds(pl.multiple_of(ref[s] * 64, 64), 64)

    @pl.loop(0, (cnt[0] + 4 * UNROLL - 1) // (4 * UNROLL))
    def _(i):
        parts = []
        for u in range(UNROLL):
            g = i * UNROLL + u
            for half in range(2):
                first = 4 * g + near * half
                second = first + far
                both = two_blocks(table[block(frm, first), :], table[block(frm, second), :])
                lhs = blocks[g, half * 64 : half * 64 + 64, :]
                prod = jnp.dot(lhs, both, preferred_element_type=F32)
                parts.append((first, prod[:, :128]))
                parts.append((second, prod[:, 128:]))
        for s, value in parts:
            acc[block(to, s), :] += value

    out[...] = acc[...].astype(BF)


def forward(count, frm, to, blocks, table):
    return pl.pallas_call(
        functools.partial(spread_kernel, 1, 2),
        out_shape=jax.ShapeDtypeStruct((8 * ND, 128), BF),
        in_specs=[SMEM, SMEM, SMEM, VMEM, VMEM],
        out_specs=VMEM,
        scratch_shapes=[pltpu.VMEM((8 * ND, 128), F32)],
        compiler_params=pltpu.CompilerParams(vmem_limit_bytes=16 << 20),
        name="forward",
    )(count, frm, to, blocks, table)


def backward_kernel(cnt, frm, to, blocks, table, hidden, out, kept, acc, sem):
    keep = pltpu.make_async_copy(hidden, kept, sem)
    keep.start()
    spread_kernel(2, 1, cnt, frm, to, blocks, table, out, acc)
    keep.wait()


def backward(count, frm, to, blocks, table, hidden):
    return pl.pallas_call(
        backward_kernel,
        out_shape=[
            jax.ShapeDtypeStruct((32 * ND, 128), BF),
            jax.ShapeDtypeStruct(hidden.shape, hidden.dtype),
        ],
        in_specs=[SMEM, SMEM, SMEM, VMEM, VMEM, ANY],
        out_specs=[VMEM, ANY],
        scratch_shapes=[pltpu.VMEM((32 * ND, 128), F32), pltpu.SemaphoreType.DMA],
        compiler_params=pltpu.CompilerParams(vmem_limit_bytes=20 << 20),
        name="backward",
    )(count, frm, to, blocks, table, hidden)


def upright(rows, width):
    eye = lax.broadcasted_iota(jnp.int32, (width, 128), 0) == lax.broadcasted_iota(
        jnp.int32, (width, 128), 1
    )
    return jnp.concatenate(
        [
            jnp.sum(jnp.where(eye, rows[i : i + 1, :], 0.0), axis=1, keepdims=True)
            for i in range(rows.shape[0])
        ],
        0,
    )


def node_kernel(
    raw_part, deg, x, ws, wn, mask, cot, zf,
    hidden, group, own_term, gsum, zt,
    yb, xsrc, rx, fsrc, fy, rd, nat, sc, grads, gr, ss, x1, y1, x2, y2, ds, gsem, ls,
):
    row, col = lax.axis_index("row"), lax.axis_index("col")
    yh, xx = col // 4, lax.rem(col, 4)
    z, side = row // 4, lax.rem(row, 4)
    zat = [lax.rem(z + e, 8) for e in range(8)]
    xat = [lax.rem(xx + e, 4) for e in range(4)]
    peers = [lax.rem(col + o, 8) for o in range(8)]
    along = [(row, yh * 4 + xat[e]) for e in range(4)]
    across = (row, (1 - yh) * 4 + xx)
    early = []

    def unmask():
        early.append(upright(mask[...].astype(F32), 128))

    greet([(row, p) for p in peers[1:]] + [(zat[e] * 4 + side, col) for e in range(1, 8)], unmask)
    send, sent = sender(ss)

    def base(e, r):
        return pl.multiple_of(((yh if r == 0 else 1 - yh) * 4 + xat[e]) * ND, ND)

    def mine(e, r, lo):
        return raw_part.at[pl.ds(base(e, r) + lo, 256)]

    ysent = {e: send(mine(e, 1, 256), yb.at[e], y1.at[e], across) for e in (2, 1, 3)}
    xsent = {}
    for part in (2, 0):
        for e in (2, 1, 3):
            src = mine(e, 1 if part == 2 else 0, 0)
            xsent[e, part] = send(src, rx.at[e - 1, part], x1.at[e - 1, part], along[e])
            if part == 2 and e == 2:
                ysent[0] = send(mine(0, 1, 256), yb.at[0], y1.at[0], across)
    degs = []
    for o in range(1, 8):
        src = deg.at[pl.ds(pl.multiple_of(peers[o] * 8, 8), 8)]
        degs.append(send(src, rd.at[o], ds.at[o], (row, peers[o])))

    def pass_on(e):
        ysent[e].wait_recv()
        xsrc[e - 1] = (mine(e, 0, 256)[...].astype(F32) + yb[e].astype(F32)).astype(BF)
        xsent[e, 1] = send(xsrc.at[e - 1], rx.at[e - 1, 1], x1.at[e - 1, 1], along[e])

    def final(part, total):
        for e in (2, 1, 3):
            xsent[e, part].wait_recv()
            total = total + rx[e - 1, part].astype(F32)
        return total

    pass_on(2)
    pass_on(1)
    pass_on(3)
    fsrc[...] = final(2, mine(0, 1, 0)[...].astype(F32)).astype(BF)
    last = send(fsrc, fy, y1.at[4], across)
    rd[0] = deg[pl.ds(pl.multiple_of(col * 8, 8), 8), :]
    keep = early[0]
    for cp in degs:
        cp.wait_recv()
    inverse = 1.0 / upright(jnp.sum(rd[...], axis=0), 64)
    nt = (((1,), (1,)), ((), ()))
    tn = (((0,), (0,)), ((), ()))
    halves = {}

    def layer(lo, raw):
        at = pl.ds(lo, 256)
        raw = raw.reshape(4, 2, 32, 128)
        for p in range(2):
            nat[pl.ds(lo + p, 128, stride=2), :] = raw[:, p].reshape(128, 128)
        inv = inverse[lo : lo + 256]
        agg = (nat[at, :] * inv).astype(BF)
        feats = x[at, :]
        pre = jnp.dot(feats, ws[...], preferred_element_type=F32)
        pre = pre + jnp.dot(agg, wn[...], preferred_element_type=F32)
        sig = jax.nn.sigmoid(pre)
        slope = sig * (1.0 + pre * (1.0 - sig))
        dpre = (cot[at, :].astype(F32) * keep[lo : lo + 256] * slope).astype(BF)
        nat[at, :] = lax.dot_general(dpre, wn[...], nt, preferred_element_type=F32) * inv
        for p in range(2):
            part = nat[pl.ds(lo + p, 128, stride=2), :].astype(BF).reshape(4, 32, 128)
            for i in range(4):
                sc[lo + i * 64 + p * 32 : lo + i * 64 + p * 32 + 32, :] = part[i]
        hidden[at, :] = (pre * sig).astype(BF)
        halves[lo] = feats, agg, dpre

    slices = []

    def later():
        g_self, g_neigh = 0.0, 0.0
        for lo, (feats, agg, dpre) in halves.items():
            own_term[lo : lo + 256, :] = lax.dot_general(dpre, ws[...], nt, preferred_element_type=F32)
            g_self = g_self + lax.dot_general(feats, dpre, tn, preferred_element_type=F32)
            g_neigh = g_neigh + lax.dot_general(agg, dpre, tn, preferred_element_type=F32)
        for i, v in enumerate((g_self[:, :128], g_self[:, 128:], g_neigh[:, :128], g_neigh[:, 128:])):
            grads[i * 128 : i * 128 + 128, :] = v.astype(BF)
        for e in range(1, 8):
            src = grads.at[pl.ds(pl.multiple_of(zat[e] * 64, 64), 64)]
            slices.append(send(src, gr.at[e], gsem.at[e], (zat[e] * 4 + side, col)))

    turned = [0]

    def turn(n):
        lo = turned[0]
        turned[0] += n

        @pl.loop(lo, lo + n)
        def _(i):
            zt[i] = zf[i].T

    stay = pltpu.make_async_copy(sc, group.at[pl.ds(base(0, 0), ND)], ls)

    def idle(when):
        if when == "B":
            ysent[0].wait_recv()
            layer(256, final(1, mine(0, 0, 256)[...].astype(F32) + yb[0].astype(F32)))
        elif when == "A":
            first = final(0, mine(0, 0, 0)[...].astype(F32))
            last.wait_recv()
            layer(0, first + fy[...].astype(F32))
        elif when == "sent":
            stay.start()
            turn(48)
        elif when == "partner":
            turn(8)
        else:
            later()
            turn(128 - 56)

    star_gather(sc, group, base, send, x2, y2, along, across, idle)
    total = grads[pl.ds(pl.multiple_of(z * 64, 64), 64), :].astype(F32)
    for e in range(1, 8):
        slices[e - 1].wait_recv()
        total = total + gr[e].astype(F32)
    gsum[...] = total
    stay.wait()
    for cp in sent:
        cp.wait_send()


def node(raw_part, deg, x, ws, wn, mask, cot, zf):
    return pl.pallas_call(
        node_kernel,
        out_shape=[
            jax.ShapeDtypeStruct((ND, 256), BF),
            jax.ShapeDtypeStruct((8 * ND, 128), BF),
            jax.ShapeDtypeStruct((ND, 128), F32),
            jax.ShapeDtypeStruct((64, 128), F32),
            jax.ShapeDtypeStruct((128, 128, 128), BF),
        ],
        in_specs=[VMEM] * 8,
        out_specs=[VMEM, ANY, VMEM, VMEM, VMEM],
        scratch_shapes=[
            pltpu.VMEM((4, 256, 128), BF),
            pltpu.VMEM((3, 256, 128), BF),
            pltpu.VMEM((3, 3, 256, 128), BF),
            pltpu.VMEM((256, 128), BF),
            pltpu.VMEM((256, 128), BF),
            pltpu.VMEM((8, 8, 128), F32),
            pltpu.VMEM((ND, 128), F32),
            pltpu.VMEM((ND, 128), BF),
            pltpu.VMEM((512, 128), BF),
            pltpu.VMEM((8, 64, 128), BF),
            pltpu.SemaphoreType.DMA((60,)),
            pltpu.SemaphoreType.DMA((3, 3)),
            pltpu.SemaphoreType.DMA((5,)),
            pltpu.SemaphoreType.DMA((3, 3)),
            pltpu.SemaphoreType.DMA((5,)),
            pltpu.SemaphoreType.DMA((8,)),
            pltpu.SemaphoreType.DMA((8,)),
            pltpu.SemaphoreType.DMA,
        ],
        compiler_params=pltpu.CompilerParams(
            collective_id=1, has_side_effects=True, vmem_limit_bytes=20 << 20
        ),
        name="node",
    )(raw_part, deg, x, ws, wn, mask, cot, zf)


def in_order(parts, me, n):
    total = None
    for p in range(n):
        i = lax.rem(me - p - 1 + 2 * n, n)
        total = parts[i] if total is None else total + parts[i]
    return total


def scatter_kernel(
    t, own_term, gpart,
    out, grad_self, grad_neigh,
    sib, ysrc, yb, zsrc, rz, fsrc, fy, gk, gx, gy, gsrc, gall,
    ss, zs, ys, ks, q0, q1, q2, q3,
):
    z, yl, k, col = place()

    def dev(zz, yy, kk, cc=None):
        return (zz * 4 + yy * 2 + kk, col if cc is None else cc)

    zat = [lax.rem(z + e, 8) for e in range(8)]
    yh, xx = col // 4, lax.rem(col, 4)
    along = (dev(zat[7], yl, k), dev(zat[1], yl, k))
    across, sibling = dev(z, 1 - yl, k), dev(z, yl, 1 - k)
    far = (1 - yh) * 4 + xx
    ypeers = (across, dev(z, yl, k, far), dev(z, 1 - yl, k, far))
    xpeers = [dev(z, yl, k, yh * 4 + lax.rem(xx + e, 4)) for e in (1, 2, 3)]
    zpeers = [dev(zat[e], yl, k) for e in range(1, 8)]
    greet([sibling, *ypeers, *xpeers, *zpeers])
    send, sent = sender(ss)
    theirs = pl.ds(pl.multiple_of((1 - k) * 32, 32), 32)
    ours = pl.ds(pl.multiple_of(k * 32, 32), 32)
    halves = send(gpart.at[theirs], gk, q0.at[0], sibling)

    sibs = {}
    for e in (4, 3, 5, 2, 6, 1, 7, 0):
        sibs[e] = send(t.at[zat[e], :, 1 - k], sib.at[e], ks.at[e], sibling)
    ready = set()

    def mine(e, r, lo, n):
        if e not in ready:
            sibs[e].wait_recv()
            ready.add(e)
        yy = yl if r == 0 else 1 - yl
        at = pl.ds(lo, n)
        return t[zat[e], yy, k, at, :].astype(F32) + sib[e, yy, at, :].astype(F32)

    ysent = {}

    def cross(e):
        ysrc[e] = mine(e, 1, 256, 256).astype(BF)
        ysent[e] = send(ysrc.at[e], yb.at[e], ys.at[e], across)

    crossed = set()

    def value(e, part, lo, n):
        if part == 2:
            return mine(e, 1, lo, n)
        if part == 0:
            return mine(e, 0, lo, n)
        if e not in crossed:
            ysent[e].wait_recv()
            crossed.add(e)
        return mine(e, 0, 256 + lo, n) + yb[e, lo : lo + n, :].astype(F32)

    piece, final = ring_reduce(4, value, lambda *a: None, zsrc, rz, send, zs, along)

    cross(4)
    piece(0, 4, 2)
    piece(1, 4, 2)
    piece(0, 4, 0)
    cross(3)
    cross(5)
    piece(1, 4, 1)
    cross(2)
    cross(6)
    cross(1)
    cross(7)
    cross(0)
    halves.wait_recv()
    gsrc[0] = gpart[pl.ds(pl.multiple_of(k * 32, 32), 32), :] + gk[...]
    swaps = [send(gsrc.at[0], gx.at[i], q1.at[i], xpeers[i]) for i in range(3)]
    for part in (2, 0, 1):
        for d in range(2):
            piece(d, 3, part)
    gx[3] = gsrc[0]
    for cp in swaps:
        cp.wait_recv()
    gsrc[1] = in_order(gx, xx, 4)
    swaps = [send(gsrc.at[1], gy.at[i], q2.at[i], ypeers[i]) for i in range(3)]
    for part in (2, 0, 1):
        for d in range(2):
            piece(d, 2, part)
    for cp in swaps:
        cp.wait_recv()
    total = (gsrc[1] + gy[0]) + (gy[1] + gy[2])
    mine_at = gall.at[z, k]
    gall[z, k] = total.astype(BF)
    swaps = [send(mine_at, mine_at, q3.at[i], zpeers[i]) for i in range(7)]
    for part in (2, 0, 1):
        for d in range(2):
            piece(d, 1, part)
    fsrc[...] = final(2).astype(BF)
    last = send(fsrc, fy, ys.at[8], across)
    first = final(0) + own_term[:256, :]
    out[256:, :] = (final(1) + own_term[256:, :]).astype(BF)
    for cp in swaps:
        cp.wait_recv()
    other = send(gall.at[:, k], gall.at[:, k], q0.at[1], sibling)
    last.wait_recv()
    out[:256, :] = (first + fy[...].astype(F32)).astype(BF)
    other.wait_recv()
    for i, ref in enumerate((grad_self, grad_neigh)):
        for h in range(2):
            lo = i * 4 + h * 2
            ref[:, h * 128 : h * 128 + 128] = gall[lo : lo + 2].astype(F32).reshape(128, 128)
    for cp in sent:
        cp.wait_send()


def scatter_rows(t, own_term, grads):
    return pl.pallas_call(
        scatter_kernel,
        out_shape=[
            jax.ShapeDtypeStruct((ND, 128), BF),
            jax.ShapeDtypeStruct((128, 256), F32),
            jax.ShapeDtypeStruct((128, 256), F32),
        ],
        in_specs=[VMEM, VMEM, VMEM],
        out_specs=[VMEM, VMEM, VMEM],
        scratch_shapes=[
            pltpu.VMEM((8, 2, ND, 128), BF),
            pltpu.VMEM((8, 256, 128), BF),
            pltpu.VMEM((8, 256, 128), BF),
            pltpu.VMEM((2, 4, 768, 128), BF),
            pltpu.VMEM((2, 4, 768, 128), BF),
            pltpu.VMEM((256, 128), BF),
            pltpu.VMEM((256, 128), BF),
            pltpu.VMEM((32, 128), F32),
            pltpu.VMEM((4, 32, 128), F32),
            pltpu.VMEM((3, 32, 128), F32),
            pltpu.VMEM((2, 32, 128), F32),
            pltpu.VMEM((8, 2, 32, 128), BF),
            pltpu.SemaphoreType.DMA((90,)),
            pltpu.SemaphoreType.DMA((2, 4, 3)),
            pltpu.SemaphoreType.DMA((9,)),
            pltpu.SemaphoreType.DMA((8,)),
            pltpu.SemaphoreType.DMA((2,)),
            pltpu.SemaphoreType.DMA((3,)),
            pltpu.SemaphoreType.DMA((3,)),
            pltpu.SemaphoreType.DMA((7,)),
        ],
        compiler_params=pltpu.CompilerParams(
            collective_id=2, has_side_effects=True, vmem_limit_bytes=20 << 20
        ),
        name="scatter_rows",
    )(t.reshape(8, 2, 2, ND, 128), own_term, grads)


def finish_kernel(*refs):
    n = len(refs) // 2
    sem = refs[-1]
    copies = [pltpu.make_async_copy(refs[i], refs[n + i], sem.at[i]) for i in range(n)]
    for cp in copies:
        cp.start()
    for cp in copies:
        cp.wait()


def finish(*arrays):
    return pl.pallas_call(
        finish_kernel,
        out_shape=[jax.ShapeDtypeStruct(a.shape, a.dtype) for a in arrays],
        in_specs=[VMEM] * len(arrays),
        out_specs=[ANY] * len(arrays),
        scratch_shapes=[pltpu.SemaphoreType.DMA((len(arrays),))],
        compiler_params=pltpu.CompilerParams(vmem_limit_bytes=16 << 20),
        name="finish",
    )(*arrays)


def shards(
    features,
    self_weight,
    neigh_weight,
    block_row,
    block_col,
    block_count,
    edge_weight,
    train_mask,
    out_cotangent,
):
    rows = block_row.reshape(512)
    cols = block_col.reshape(512)
    count = block_count.reshape(1)
    mask = train_mask.reshape(4, 128)
    gathered, zf, deg = gather_rows(
        count, block_row.reshape(1, 512), features, edge_weight.reshape(512, 4096)
    )
    raw_part = forward(count, cols, rows, zf, gathered)
    hidden, group, own_term, grads, zt = node(
        raw_part, deg, features, self_weight, neigh_weight, mask, out_cotangent, zf
    )
    through, hidden = backward(count, rows, cols, zt, group, hidden)
    return hidden, *finish(*scatter_rows(through, own_term, grads))


def solution(mesh):
    in_specs = (
        P(("row", "col"), None),
        P(),
        P(),
        P("row", "col", None),
        P("row", "col", None),
        P("row", "col"),
        P("row", "col", None, None),
        P(("row", "col")),
        P(("row", "col"), None),
    )
    out_specs = (P(("row", "col"), None), P(("row", "col"), None), P(), P())
    return jax.shard_map(shards, mesh=mesh, in_specs=in_specs, out_specs=out_specs, check_vma=False)
```

```python
import functools

import jax
import jax.numpy as jnp
from jax import lax
from jax.experimental import pallas as pl
from jax.experimental.pallas import tpu as pltpu
from jax.sharding import PartitionSpec as P

MESH = pl.DeviceIdType.MESH
BF = jnp.bfloat16
F32 = jnp.float32
VMEM = pl.BlockSpec(memory_space=pltpu.VMEM)
SMEM = pl.BlockSpec(memory_space=pltpu.SMEM)
ANY = pl.BlockSpec(memory_space=pl.ANY)
ND = 512
UNROLL = 32
WORK = (8, 3, 3, 3, 1)
TURN = (32,)


def place():
    row = lax.axis_index("row")
    return row // 4, (row // 2) % 2, row % 2, lax.axis_index("col")


def greet(targets, meanwhile=None):
    barrier = pltpu.get_barrier_semaphore()
    for target in targets:
        pl.semaphore_signal(barrier, inc=1, device_id=target, device_id_type=MESH)
    if meanwhile is not None:
        meanwhile()
    pl.semaphore_wait(barrier, len(targets))


def sender(ss):
    sent = []

    def send(src, dst, sem, target):
        cp = pltpu.make_async_remote_copy(
            src_ref=src,
            dst_ref=dst,
            send_sem=ss.at[len(sent)],
            recv_sem=sem,
            device_id=target,
            device_id_type=MESH,
        )
        cp.start()
        sent.append(cp)
        return cp

    return send, sent


def ring_gather(half, x, table, base, send, zs, ys, along, across, share, idle):
    last = {}

    def go(src, row, lo, n, sem, target):
        return send(
            x.at[pl.ds(lo, n)] if src is x else table.at[pl.ds(row + lo, n)],
            table.at[pl.ds(row + lo, n)],
            sem,
            target,
        )

    own, partner = base(0, 0), base(0, 1)
    first = [go(x, own, 128 * i, 128, ys.at[0, i], across) for i in range(2)]
    for part in (1, 0):
        for i in range(2):
            for d in range(2):
                lo = part * 256 + i * 128
                last[d, 1, part, i] = go(x, own, lo, 128, zs.at[d, 0, part, i], along[d])
    crossing = [([go(x, own, 256, 256, ys.at[1, 0], across)], partner)]
    share(x, own, 0, 512)
    idle(0)
    for i in range(2):
        first[i].wait_recv()
        for d in range(2):
            last[d, 1, 2, i] = go(table, partner, 128 * i, 128, zs.at[d, 0, 2, i], along[d])
    for step in range(1, half + 1):
        arriving, crossing = crossing, []
        crossed = ([], [])
        for part, i in ((1, 0), (1, 1), (2, 0), (2, 1), (0, 0), (0, 1)):
            for d in range(2):
                if (d, step, part, i) not in last:
                    continue
                e = 2 * half - step if d == 0 else step
                row = base(e, 0 if part < 2 else 1)
                lo = (0, 256, 0)[part] + 128 * i
                last[d, step, part, i].wait_recv()
                goes = step < half - 1
                if step == half - 1:
                    goes = part == d or (part == 2 and i == d)
                if goes:
                    last[d, step + 1, part, i] = go(
                        table, row, lo, 128, zs.at[d, step, part, i], along[d]
                    )
                if part == 1:
                    cp = go(table, row, lo, 128, ys.at[2 * step + d, i], across)
                    crossed[d].append(cp)
                    if i == 1:
                        crossing.append((crossed[d], base(e, 1)))
                if step == half:
                    share(table, row, lo, 128)
                elif part == 0 and i == 1:
                    share(table, row, 0, 512)
            idle(step)
        for cps, row in arriving:
            for cp in cps:
                cp.wait_recv()
            share(table, row, 0, 512)
    for cps, row in crossing:
        for i, cp in enumerate(cps):
            cp.wait_recv()
            share(table, row, 256 + 128 * i, 128)


def star_gather(x, table, base, send, xs, ys, along, across, idle):
    def go(src, row, lo, sem, target):
        return send(
            x.at[pl.ds(lo, 256)] if src is x else table.at[pl.ds(row + lo, 256)],
            table.at[pl.ds(row + lo, 256)],
            sem,
            target,
        )

    own, partner = base(0, 0), base(0, 1)
    idle("B")
    second = [go(x, own, 256, xs.at[e - 1, 1], along[e]) for e in (1, 3, 2)]
    rest = [go(x, own, 256, ys.at[0], across)]
    idle("A")
    first = go(x, own, 0, ys.at[4], across)
    rest += [go(x, own, 0, xs.at[e - 1, 0], along[e]) for e in (1, 3, 2)]
    idle("sent")
    first.wait_recv()
    rest += [go(table, partner, 0, xs.at[e - 1, 2], along[e]) for e in (1, 3, 2)]
    idle("partner")
    for cp, e in zip(second, (1, 3, 2)):
        cp.wait_recv()
        rest.append(go(table, base(4 - e, 0), 256, ys.at[e], across))
    idle("last")
    for cp in rest:
        cp.wait_recv()


def ring_reduce(half, value, direct, zsrc, rz, send, zs, along):
    zsent = {}

    def arrived(d, step, part, lo, n):
        return rz[d, step, part * 256 + lo : part * 256 + lo + n, :].astype(F32)

    def piece(d, step, part):
        e = (2 * half - step) if d == 0 else step
        lo, n = (0, 256) if (step < half or part < 2) else (d * 128, 128)
        at = pl.ds(part * 256 + lo, n)
        alone = step == half or (step == half - 1 and part == 1 - d)
        src = direct(e, part, lo, n) if alone else None
        if src is None:
            total = value(e, part, lo, n)
            if step < half - 1 or (step == half - 1 and part == d):
                zsent[d, step + 1, part].wait_recv()
                total = total + arrived(d, step, part, 0, 256)
            elif step == half - 1 and part == 2:
                zsent[d, half, 2].wait_recv()
                halves = [total[:128], total[128:]]
                halves[d] = halves[d] + arrived(d, step, 2, d * 128, 128)
                total = jnp.concatenate(halves, 0)
            zsrc[d, step - 1, at, :] = total.astype(BF)
            src = zsrc.at[d, step - 1, at]
        zsent[d, step, part] = send(src, rz.at[d, step - 1, at], zs.at[d, step - 1, part], along[d])

    def final(part):
        total = value(0, part, 0, 256)
        for d in range(2):
            zsent[d, 1, part].wait_recv()
            total = total + arrived(d, 0, part, 0, 256)
        return total

    return piece, final


def gather_kernel(
    cnt, rows_hbm, x, w,
    g, zf, deg,
    wv, rows, pat, dsl, ss, zs, ys, ks, ls, wsem,
):
    z, yl, k, col = place()

    def dev(zz, yy, kk):
        return (zz * 4 + yy * 2 + kk, col)

    along = (dev(lax.rem(z + 1, 8), yl, k), dev(lax.rem(z + 7, 8), yl, k))
    across, sibling = dev(z, 1 - yl, k), dev(z, yl, 1 - k)
    slabs = [
        pltpu.make_async_copy(w.at[pl.ds(i * 64, 64)], wv.at[pl.ds(i * 64, 64)], wsem.at[i])
        for i in range(8)
    ]
    names = pltpu.make_async_copy(rows_hbm, rows, ls.at[1])

    def fetch():
        for cp in (*slabs, names):
            cp.start()
        at = lax.broadcasted_iota(jnp.int32, (4096, 128), 0) // 64
        pat[...] = (at == lax.broadcasted_iota(jnp.int32, (4096, 128), 1)).astype(BF)

    greet((*along, across, sibling), fetch)
    send, sent = sender(ss)

    def base(e, r):
        yy = yl if r == 0 else 1 - yl
        return pl.multiple_of((lax.rem(z + e, 8) * 4 + yy * 2 + k) * ND, ND)

    to_sibling = []

    def share(src, row, lo, n):
        at = pl.ds(row + lo, n)
        src = x.at[pl.ds(lo, n)] if src is x else g.at[at]
        to_sibling.append(send(src, g.at[at], ks.at[len(to_sibling)], sibling))

    low = lax.broadcasted_iota(jnp.int32, (32, 128), 1) < 64
    lim = cnt[0]
    done = [0]

    def unit(i):
        b = pl.multiple_of(i * 8, 8)
        live = (b + lax.broadcasted_iota(jnp.int32, (8, 4096), 0)) < lim
        y = jnp.where(live, wv[pl.ds(b, 8), :], 0).astype(F32).reshape(8, 32, 128)
        for h4 in range(2):
            y4 = [y[h4 * 4 + s] for s in range(4)]
            r4 = [pltpu.roll(v, 64, 1) for v in y4]
            zf[i * 2 + h4] = jnp.concatenate(
                [
                    jnp.where(low, y4[0], r4[2]),
                    jnp.where(low, r4[0], y4[2]),
                    jnp.where(low, y4[1], r4[3]),
                    jnp.where(low, r4[1], y4[3]),
                ],
                0,
            ).astype(BF)

    def work(n):
        n = min(n, 64 - done[0])
        if n <= 0:
            return
        lo = done[0]
        for i in range(lo // 8 if lo % 8 == 0 else lo // 8 + 1, (lo + n - 1) // 8 + 1):
            slabs[i].wait()
        pl.loop(lo, lo + n)(unit)
        for i in range(lo // 8, (lo + n) // 8):
            at = pl.ds(i * 64, 64)
            dsl[at, :] = jnp.dot(
                wv[at, :].astype(F32).astype(BF), pat[...], preferred_element_type=F32
            ).astype(BF)
        done[0] += n

    def idle(step):
        work(WORK[step])

    mine = pltpu.make_async_copy(x, g.at[pl.ds(base(0, 0), ND)], ls.at[0])
    mine.start()
    ring_gather(4, x, g, base, send, zs, ys, along, across, share, idle)
    work(64)
    names.wait()
    slot = lax.broadcasted_iota(jnp.int32, (64, 512), 1)
    hot = (lax.broadcasted_iota(jnp.int32, (64, 512), 0) == rows[...]) & (slot < lim)
    deg[...] = jnp.dot(hot.astype(F32).astype(BF), dsl[...], preferred_element_type=F32)
    for cp in to_sibling:
        cp.wait_recv()
    for cp in sent:
        cp.wait_send()
    mine.wait()


def gather_rows(count, rows, x, w):
    rows = pltpu.with_memory_space_constraint(rows, pltpu.HBM)
    x = pltpu.with_memory_space_constraint(x, pltpu.HBM)
    w = pltpu.with_memory_space_constraint(w, pltpu.HBM)
    return pl.pallas_call(
        gather_kernel,
        out_shape=[
            jax.ShapeDtypeStruct((32 * ND, 128), BF),
            jax.ShapeDtypeStruct((128, 128, 128), BF),
            jax.ShapeDtypeStruct((64, 128), F32),
        ],
        in_specs=[SMEM, ANY, ANY, ANY],
        out_specs=[ANY, VMEM, VMEM],
        scratch_shapes=[
            pltpu.VMEM((512, 4096), jnp.int32),
            pltpu.VMEM((1, 512), jnp.int32),
            pltpu.VMEM((4096, 128), BF),
            pltpu.VMEM((512, 128), BF),
            pltpu.SemaphoreType.DMA((110,)),
            pltpu.SemaphoreType.DMA((2, 4, 3, 2)),
            pltpu.SemaphoreType.DMA((10, 2)),
            pltpu.SemaphoreType.DMA((40,)),
            pltpu.SemaphoreType.DMA((2,)),
            pltpu.SemaphoreType.DMA((8,)),
        ],
        compiler_params=pltpu.CompilerParams(
            collective_id=0, has_side_effects=True, vmem_limit_bytes=43 << 20
        ),
        name="gather_rows",
    )(count, rows, x, w)


def two_blocks(a, b):
    zero = jnp.zeros((64, 128), BF)
    return jnp.concatenate(
        [jnp.concatenate([a, zero], 1), jnp.concatenate([zero, b], 1)], 0
    )


def spread_kernel(near, far, cnt, frm, to, blocks, table, out, acc):
    acc[...] = jnp.zeros_like(acc)

    def block(ref, s):
        return pl.ds(pl.multiple_of(ref[s] * 64, 64), 64)

    @pl.loop(0, (cnt[0] + 4 * UNROLL - 1) // (4 * UNROLL))
    def _(i):
        parts = []
        for u in range(UNROLL):
            g = i * UNROLL + u
            for half in range(2):
                first = 4 * g + near * half
                second = first + far
                both = two_blocks(table[block(frm, first), :], table[block(frm, second), :])
                lhs = blocks[g, half * 64 : half * 64 + 64, :]
                prod = jnp.dot(lhs, both, preferred_element_type=F32)
                parts.append((first, prod[:, :128]))
                parts.append((second, prod[:, 128:]))
        for s, value in parts:
            acc[block(to, s), :] += value

    out[...] = acc[...].astype(BF)


def forward(count, frm, to, blocks, table):
    return pl.pallas_call(
        functools.partial(spread_kernel, 1, 2),
        out_shape=jax.ShapeDtypeStruct((8 * ND, 128), BF),
        in_specs=[SMEM, SMEM, SMEM, VMEM, VMEM],
        out_specs=VMEM,
        scratch_shapes=[pltpu.VMEM((8 * ND, 128), F32)],
        compiler_params=pltpu.CompilerParams(vmem_limit_bytes=16 << 20),
        name="forward",
    )(count, frm, to, blocks, table)


def backward_kernel(cnt, frm, to, blocks, table, hidden, out, kept, acc, sem):
    keep = pltpu.make_async_copy(hidden, kept, sem)
    keep.start()
    spread_kernel(2, 1, cnt, frm, to, blocks, table, out, acc)
    keep.wait()


def backward(count, frm, to, blocks, table, hidden):
    return pl.pallas_call(
        backward_kernel,
        out_shape=[
            jax.ShapeDtypeStruct((32 * ND, 128), BF),
            jax.ShapeDtypeStruct(hidden.shape, hidden.dtype),
        ],
        in_specs=[SMEM, SMEM, SMEM, VMEM, VMEM, ANY],
        out_specs=[VMEM, ANY],
        scratch_shapes=[pltpu.VMEM((32 * ND, 128), F32), pltpu.SemaphoreType.DMA],
        compiler_params=pltpu.CompilerParams(vmem_limit_bytes=20 << 20),
        name="backward",
    )(count, frm, to, blocks, table, hidden)


def upright(rows, width):
    eye = lax.broadcasted_iota(jnp.int32, (width, 128), 0) == lax.broadcasted_iota(
        jnp.int32, (width, 128), 1
    )
    return jnp.concatenate(
        [
            jnp.sum(jnp.where(eye, rows[i : i + 1, :], 0.0), axis=1, keepdims=True)
            for i in range(rows.shape[0])
        ],
        0,
    )


def node_kernel(
    raw_part, deg, x, ws, wn, mask, cot, zf,
    hidden, group, own_term, gsum, zt,
    yb, xsrc, rx, fsrc, fy, rd, nat, sc, grads, gr, ss, x1, y1, x2, y2, ds, gsem, ls,
):
    row, col = lax.axis_index("row"), lax.axis_index("col")
    yh, xx = col // 4, lax.rem(col, 4)
    z, side = row // 4, lax.rem(row, 4)
    zat = [lax.rem(z + e, 8) for e in range(8)]
    xat = [lax.rem(xx + e, 4) for e in range(4)]
    peers = [lax.rem(col + o, 8) for o in range(8)]
    along = [(row, yh * 4 + xat[e]) for e in range(4)]
    across = (row, (1 - yh) * 4 + xx)
    early = []

    def unmask():
        early.append(upright(mask[...].astype(F32), 128))

    greet([(row, p) for p in peers[1:]] + [(zat[e] * 4 + side, col) for e in range(1, 8)], unmask)
    send, sent = sender(ss)

    def base(e, r):
        return pl.multiple_of(((yh if r == 0 else 1 - yh) * 4 + xat[e]) * ND, ND)

    def mine(e, r, lo):
        return raw_part.at[pl.ds(base(e, r) + lo, 256)]

    ysent = {e: send(mine(e, 1, 256), yb.at[e], y1.at[e], across) for e in (2, 1, 3)}
    xsent = {}
    for part in (2, 0):
        for e in (2, 1, 3):
            src = mine(e, 1 if part == 2 else 0, 0)
            xsent[e, part] = send(src, rx.at[e - 1, part], x1.at[e - 1, part], along[e])
            if part == 2 and e == 2:
                ysent[0] = send(mine(0, 1, 256), yb.at[0], y1.at[0], across)
    degs = []
    for o in range(1, 8):
        src = deg.at[pl.ds(pl.multiple_of(peers[o] * 8, 8), 8)]
        degs.append(send(src, rd.at[o], ds.at[o], (row, peers[o])))

    def pass_on(e):
        ysent[e].wait_recv()
        xsrc[e - 1] = (mine(e, 0, 256)[...].astype(F32) + yb[e].astype(F32)).astype(BF)
        xsent[e, 1] = send(xsrc.at[e - 1], rx.at[e - 1, 1], x1.at[e - 1, 1], along[e])

    def final(part, total):
        for e in (2, 1, 3):
            xsent[e, part].wait_recv()
            total = total + rx[e - 1, part].astype(F32)
        return total

    turned = [0]

    def turn(n):
        lo = turned[0]
        turned[0] += n

        @pl.loop(lo, lo + n)
        def _(i):
            zt[i] = zf[i].T

    pass_on(2)
    pass_on(1)
    pass_on(3)
    fsrc[...] = final(2, mine(0, 1, 0)[...].astype(F32)).astype(BF)
    last = send(fsrc, fy, y1.at[4], across)
    turn(32)
    rd[0] = deg[pl.ds(pl.multiple_of(col * 8, 8), 8), :]
    keep = early[0]
    for cp in degs:
        cp.wait_recv()
    inverse = 1.0 / upright(jnp.sum(rd[...], axis=0), 64)
    nt = (((1,), (1,)), ((), ()))
    tn = (((0,), (0,)), ((), ()))
    halves = {}

    def layer(lo, raw):
        at = pl.ds(lo, 256)
        raw = raw.reshape(4, 2, 32, 128)
        for p in range(2):
            nat[pl.ds(lo + p, 128, stride=2), :] = raw[:, p].reshape(128, 128)
        inv = inverse[lo : lo + 256]
        agg = (nat[at, :] * inv).astype(BF)
        feats = x[at, :]
        pre = jnp.dot(feats, ws[...], preferred_element_type=F32)
        pre = pre + jnp.dot(agg, wn[...], preferred_element_type=F32)
        sig = jax.nn.sigmoid(pre)
        slope = sig * (1.0 + pre * (1.0 - sig))
        dpre = (cot[at, :].astype(F32) * keep[lo : lo + 256] * slope).astype(BF)
        nat[at, :] = lax.dot_general(dpre, wn[...], nt, preferred_element_type=F32) * inv
        for p in range(2):
            part = nat[pl.ds(lo + p, 128, stride=2), :].astype(BF).reshape(4, 32, 128)
            for i in range(4):
                sc[lo + i * 64 + p * 32 : lo + i * 64 + p * 32 + 32, :] = part[i]
        hidden[at, :] = (pre * sig).astype(BF)
        halves[lo] = feats, agg, dpre

    slices = []

    def later():
        g_self, g_neigh = 0.0, 0.0
        for lo, (feats, agg, dpre) in halves.items():
            own_term[lo : lo + 256, :] = lax.dot_general(dpre, ws[...], nt, preferred_element_type=F32)
            g_self = g_self + lax.dot_general(feats, dpre, tn, preferred_element_type=F32)
            g_neigh = g_neigh + lax.dot_general(agg, dpre, tn, preferred_element_type=F32)
        for i, v in enumerate((g_self[:, :128], g_self[:, 128:], g_neigh[:, :128], g_neigh[:, 128:])):
            grads[i * 128 : i * 128 + 128, :] = v.astype(BF)
        for e in range(1, 8):
            src = grads.at[pl.ds(pl.multiple_of(zat[e] * 64, 64), 64)]
            slices.append(send(src, gr.at[e], gsem.at[e], (zat[e] * 4 + side, col)))

    stay = pltpu.make_async_copy(sc, group.at[pl.ds(base(0, 0), ND)], ls)

    def idle(when):
        if when == "B":
            ysent[0].wait_recv()
            layer(256, final(1, mine(0, 0, 256)[...].astype(F32) + yb[0].astype(F32)))
        elif when == "A":
            first = final(0, mine(0, 0, 0)[...].astype(F32))
            last.wait_recv()
            layer(0, first + fy[...].astype(F32))
        elif when == "sent":
            stay.start()
            turn(48)
        elif when == "partner":
            turn(8)
        else:
            later()
            turn(128 - 88)

    star_gather(sc, group, base, send, x2, y2, along, across, idle)
    total = grads[pl.ds(pl.multiple_of(z * 64, 64), 64), :].astype(F32)
    for e in range(1, 8):
        slices[e - 1].wait_recv()
        total = total + gr[e].astype(F32)
    gsum[...] = total
    stay.wait()
    for cp in sent:
        cp.wait_send()


def node(raw_part, deg, x, ws, wn, mask, cot, zf):
    return pl.pallas_call(
        node_kernel,
        out_shape=[
            jax.ShapeDtypeStruct((ND, 256), BF),
            jax.ShapeDtypeStruct((8 * ND, 128), BF),
            jax.ShapeDtypeStruct((ND, 128), F32),
            jax.ShapeDtypeStruct((64, 128), F32),
            jax.ShapeDtypeStruct((128, 128, 128), BF),
        ],
        in_specs=[VMEM] * 8,
        out_specs=[VMEM, ANY, VMEM, VMEM, VMEM],
        scratch_shapes=[
            pltpu.VMEM((4, 256, 128), BF),
            pltpu.VMEM((3, 256, 128), BF),
            pltpu.VMEM((3, 3, 256, 128), BF),
            pltpu.VMEM((256, 128), BF),
            pltpu.VMEM((256, 128), BF),
            pltpu.VMEM((8, 8, 128), F32),
            pltpu.VMEM((ND, 128), F32),
            pltpu.VMEM((ND, 128), BF),
            pltpu.VMEM((512, 128), BF),
            pltpu.VMEM((8, 64, 128), BF),
            pltpu.SemaphoreType.DMA((60,)),
            pltpu.SemaphoreType.DMA((3, 3)),
            pltpu.SemaphoreType.DMA((5,)),
            pltpu.SemaphoreType.DMA((3, 3)),
            pltpu.SemaphoreType.DMA((5,)),
            pltpu.SemaphoreType.DMA((8,)),
            pltpu.SemaphoreType.DMA((8,)),
            pltpu.SemaphoreType.DMA,
        ],
        compiler_params=pltpu.CompilerParams(
            collective_id=1, has_side_effects=True, vmem_limit_bytes=20 << 20
        ),
        name="node",
    )(raw_part, deg, x, ws, wn, mask, cot, zf)


def in_order(parts, me, n):
    total = None
    for p in range(n):
        i = lax.rem(me - p - 1 + 2 * n, n)
        total = parts[i] if total is None else total + parts[i]
    return total


def scatter_kernel(
    t, own_term, gpart,
    out, grad_self, grad_neigh,
    sib, ysrc, yb, zsrc, rz, fsrc, fy, gk, gx, gy, gsrc, gall,
    ss, zs, ys, ks, q0, q1, q2, q3,
):
    z, yl, k, col = place()

    def dev(zz, yy, kk, cc=None):
        return (zz * 4 + yy * 2 + kk, col if cc is None else cc)

    zat = [lax.rem(z + e, 8) for e in range(8)]
    yh, xx = col // 4, lax.rem(col, 4)
    along = (dev(zat[7], yl, k), dev(zat[1], yl, k))
    across, sibling = dev(z, 1 - yl, k), dev(z, yl, 1 - k)
    far = (1 - yh) * 4 + xx
    ypeers = (across, dev(z, yl, k, far), dev(z, 1 - yl, k, far))
    xpeers = [dev(z, yl, k, yh * 4 + lax.rem(xx + e, 4)) for e in (1, 2, 3)]
    zpeers = [dev(zat[e], yl, k) for e in range(1, 8)]
    greet([sibling, *ypeers, *xpeers, *zpeers])
    send, sent = sender(ss)
    theirs = pl.ds(pl.multiple_of((1 - k) * 32, 32), 32)
    ours = pl.ds(pl.multiple_of(k * 32, 32), 32)
    halves = send(gpart.at[theirs], gk, q0.at[0], sibling)

    sibs = {}
    for e in (4, 3, 5, 2, 6, 1, 7, 0):
        sibs[e] = send(t.at[zat[e], :, 1 - k], sib.at[e], ks.at[e], sibling)
    ready = set()

    def mine(e, r, lo, n):
        if e not in ready:
            sibs[e].wait_recv()
            ready.add(e)
        yy = yl if r == 0 else 1 - yl
        at = pl.ds(lo, n)
        return t[zat[e], yy, k, at, :].astype(F32) + sib[e, yy, at, :].astype(F32)

    ysent = {}

    def cross(e):
        ysrc[e] = mine(e, 1, 256, 256).astype(BF)
        ysent[e] = send(ysrc.at[e], yb.at[e], ys.at[e], across)

    crossed = set()

    def value(e, part, lo, n):
        if part == 2:
            return mine(e, 1, lo, n)
        if part == 0:
            return mine(e, 0, lo, n)
        if e not in crossed:
            ysent[e].wait_recv()
            crossed.add(e)
        return mine(e, 0, 256 + lo, n) + yb[e, lo : lo + n, :].astype(F32)

    piece, final = ring_reduce(4, value, lambda *a: None, zsrc, rz, send, zs, along)

    cross(4)
    piece(0, 4, 2)
    piece(1, 4, 2)
    piece(0, 4, 0)
    cross(3)
    cross(5)
    piece(1, 4, 1)
    cross(2)
    cross(6)
    cross(1)
    cross(7)
    cross(0)
    halves.wait_recv()
    gsrc[0] = gpart[pl.ds(pl.multiple_of(k * 32, 32), 32), :] + gk[...]
    swaps = [send(gsrc.at[0], gx.at[i], q1.at[i], xpeers[i]) for i in range(3)]
    for part in (2, 0, 1):
        for d in range(2):
            piece(d, 3, part)
    gx[3] = gsrc[0]
    for cp in swaps:
        cp.wait_recv()
    gsrc[1] = in_order(gx, xx, 4)
    swaps = [send(gsrc.at[1], gy.at[i], q2.at[i], ypeers[i]) for i in range(3)]
    for part in (2, 0, 1):
        for d in range(2):
            piece(d, 2, part)
    for cp in swaps:
        cp.wait_recv()
    total = (gsrc[1] + gy[0]) + (gy[1] + gy[2])
    mine_at = gall.at[z, k]
    gall[z, k] = total.astype(BF)
    swaps = [send(mine_at, mine_at, q3.at[i], zpeers[i]) for i in range(7)]
    for part in (2, 0, 1):
        for d in range(2):
            piece(d, 1, part)
    fsrc[...] = final(2).astype(BF)
    last = send(fsrc, fy, ys.at[8], across)
    first = final(0) + own_term[:256, :]
    out[256:, :] = (final(1) + own_term[256:, :]).astype(BF)
    for cp in swaps:
        cp.wait_recv()
    other = send(gall.at[:, k], gall.at[:, k], q0.at[1], sibling)
    last.wait_recv()
    out[:256, :] = (first + fy[...].astype(F32)).astype(BF)
    other.wait_recv()
    for i, ref in enumerate((grad_self, grad_neigh)):
        for h in range(2):
            lo = i * 4 + h * 2
            ref[:, h * 128 : h * 128 + 128] = gall[lo : lo + 2].astype(F32).reshape(128, 128)
    for cp in sent:
        cp.wait_send()


def scatter_rows(t, own_term, grads):
    return pl.pallas_call(
        scatter_kernel,
        out_shape=[
            jax.ShapeDtypeStruct((ND, 128), BF),
            jax.ShapeDtypeStruct((128, 256), F32),
            jax.ShapeDtypeStruct((128, 256), F32),
        ],
        in_specs=[VMEM, VMEM, VMEM],
        out_specs=[VMEM, VMEM, VMEM],
        scratch_shapes=[
            pltpu.VMEM((8, 2, ND, 128), BF),
            pltpu.VMEM((8, 256, 128), BF),
            pltpu.VMEM((8, 256, 128), BF),
            pltpu.VMEM((2, 4, 768, 128), BF),
            pltpu.VMEM((2, 4, 768, 128), BF),
            pltpu.VMEM((256, 128), BF),
            pltpu.VMEM((256, 128), BF),
            pltpu.VMEM((32, 128), F32),
            pltpu.VMEM((4, 32, 128), F32),
            pltpu.VMEM((3, 32, 128), F32),
            pltpu.VMEM((2, 32, 128), F32),
            pltpu.VMEM((8, 2, 32, 128), BF),
            pltpu.SemaphoreType.DMA((90,)),
            pltpu.SemaphoreType.DMA((2, 4, 3)),
            pltpu.SemaphoreType.DMA((9,)),
            pltpu.SemaphoreType.DMA((8,)),
            pltpu.SemaphoreType.DMA((2,)),
            pltpu.SemaphoreType.DMA((3,)),
            pltpu.SemaphoreType.DMA((3,)),
            pltpu.SemaphoreType.DMA((7,)),
        ],
        compiler_params=pltpu.CompilerParams(
            collective_id=2, has_side_effects=True, vmem_limit_bytes=20 << 20
        ),
        name="scatter_rows",
    )(t.reshape(8, 2, 2, ND, 128), own_term, grads)


def finish_kernel(*refs):
    n = len(refs) // 2
    sem = refs[-1]
    copies = [pltpu.make_async_copy(refs[i], refs[n + i], sem.at[i]) for i in range(n)]
    for cp in copies:
        cp.start()
    for cp in copies:
        cp.wait()


def finish(*arrays):
    return pl.pallas_call(
        finish_kernel,
        out_shape=[jax.ShapeDtypeStruct(a.shape, a.dtype) for a in arrays],
        in_specs=[VMEM] * len(arrays),
        out_specs=[ANY] * len(arrays),
        scratch_shapes=[pltpu.SemaphoreType.DMA((len(arrays),))],
        compiler_params=pltpu.CompilerParams(vmem_limit_bytes=16 << 20),
        name="finish",
    )(*arrays)


def shards(
    features,
    self_weight,
    neigh_weight,
    block_row,
    block_col,
    block_count,
    edge_weight,
    train_mask,
    out_cotangent,
):
    rows = block_row.reshape(512)
    cols = block_col.reshape(512)
    count = block_count.reshape(1)
    mask = train_mask.reshape(4, 128)
    gathered, zf, deg = gather_rows(
        count, block_row.reshape(1, 512), features, edge_weight.reshape(512, 4096)
    )
    raw_part = forward(count, cols, rows, zf, gathered)
    hidden, group, own_term, grads, zt = node(
        raw_part, deg, features, self_weight, neigh_weight, mask, out_cotangent, zf
    )
    through, hidden = backward(count, rows, cols, zt, group, hidden)
    return hidden, *finish(*scatter_rows(through, own_term, grads))


def solution(mesh):
    in_specs = (
        P(("row", "col"), None),
        P(),
        P(),
        P("row", "col", None),
        P("row", "col", None),
        P("row", "col"),
        P("row", "col", None, None),
        P(("row", "col")),
        P(("row", "col"), None),
    )
    out_specs = (P(("row", "col"), None), P(("row", "col"), None), P(), P())
    return jax.shard_map(shards, mesh=mesh, in_specs=in_specs, out_specs=out_specs, check_vma=False)
```
